32 devices in a mesh: grp: 2 (over x), rank: 16 (over z, y, core).
Axes of the slice: x: 2, y: 2, z: 4, core: 2. Of those that a mesh axis runs over, the one named last changes fastest.
Arguments:
- multipole: bfloat16 [888, 8192], P(None, ('grp', 'rank')), may hold values from -6 to 6
- compress: bfloat16 [256, 888], replicated, may hold values from -0.1875 to 0.1875
- expand: bfloat16 [888, 256], replicated, may hold values from -0.375 to 0.375
- octant_ops: bfloat16 [8, 256, 256], replicated, may hold values from -0.125 to 0.125
- far_ops: bfloat16 [16, 256, 256], replicated, may hold values from -0.1875 to 0.1875
- list_seven: int32 [16, 8192], P(None, ('grp', 'rank')), may hold values from -1 to 8191, as said below
- list_six: int32 [16, 1024], P(None, ('grp', 'rank')), may hold values from -1 to 1023, as said below
- list_five: int32 [16, 128], P(None, ('grp', 'rank')), may hold values from -1 to 127, as said below
- list_four: int32 [16, 16], replicated, may hold values from -1 to 15, as said below
- list_three: int32 [16, 2], replicated, may hold values from -1 to 1, as said below
Outputs:
- potential_coef: float32 [888, 8192], P(None, ('grp', 'rank'))
The draws below stay inside these ranges and needn't reach their ends.
Inputs may be any that keep to these rules, and one draw needn't show every extreme that they name: `list_seven`: entry [c, t] is the source box of box t of the finest level for class c, or -1; a source differs from its target by at most 256. `list_six`: as list_seven for the second finest level; a source differs from its target by at most 32. `list_five`: as list_seven for the third finest level; a source differs from its target by at most 4. `list_four`: entry [c, t] is the source box of box t for class c, or -1. `list_three`: entry [c, t] is the source box of box t for class c, or -1.
All inputs are finite; a program needn't handle non-finite values.
Results may differ from the reference program's by a relative error of at most 0.0085.
Values may be sent and summed in bfloat16 or wider, within the bound.
A program may use at most 64 MiB of HBM per device.

```python
import jax
import jax.numpy as jnp
from jax import lax

S = 888
R = 256
CLS = 16
BOX_DEV = 256
NB = 8192
NB6 = 1024
NB5 = 128
NB4 = 16
NB3 = 2


def make_list(key, count, span):
    first, second = jax.random.split(key)
    target = jnp.arange(count, dtype=jnp.int32)[None, :]
    offsets = jax.random.randint(first, (CLS, count), -span, span + 1)
    living = jax.random.randint(second, (CLS, count), 0, 4) > 0
    source = target + offsets
    valid = living & (source >= 0) & (source < count)
    result = jnp.where(valid, source, -1).astype(jnp.int32)
    result = result.at[0, count - 1].set(count - 1)
    result = result.at[1, 0].set(min(span, count - 1))
    result = result.at[CLS - 1, 0].set(-1)
    return result


def draw_list_seven(key, part):
    return make_list(jax.random.fold_in(key, 7), NB, BOX_DEV)


def draw_list_six(key, part):
    return make_list(jax.random.fold_in(key, 6), NB6, BOX_DEV // 8)


def draw_list_five(key, part):
    return make_list(jax.random.fold_in(key, 5), NB5, BOX_DEV // 64)


def draw_list_four(key, part):
    return make_list(jax.random.fold_in(key, 4), NB4, NB4)


def draw_list_three(key, part):
    return make_list(jax.random.fold_in(key, 3), NB3, NB3)


def block_levels(rng, shape, shards, low, top_value):
    def one(axis_at, parts):
        heights = jax.random.uniform(jax.random.fold_in(jax.random.fold_in(rng, 6), axis_at), (parts,), jnp.float32, low / len(shards), top_value / len(shards))
        return jnp.repeat(jnp.exp(heights), shape[axis_at] // parts).reshape((-1,) + (1,) * (len(shape) - axis_at - 1))

    gain = one(*shards[0])
    for cut in shards[1:]:
        gain = gain * one(*cut)
    return gain


def centred(own_key, extent, deviation, bound, cuts=(), kind=jnp.bfloat16):
    drawn = jax.random.normal(own_key, extent, jnp.float32) * deviation
    if len(cuts) > 0:
        drawn = block_levels(own_key, extent, cuts, -0.22, 0.18) * drawn
    return jnp.clip(drawn, min=-bound, max=bound).astype(kind)


def setup_inputs(seed: int = 0) -> dict:
    splits = jax.random.split(jax.random.key(seed), 11)
    return {
        "multipole": centred(splits[0], (S, NB), 1.0, 6.0, ((1, 32),)),
        "compress": centred(splits[1], (R, S), S ** -0.5, 0.1875),
        "expand": centred(splits[2], (S, R), R ** -0.5, 0.375),
        "octant_ops": centred(splits[3], (8, R, R), (8 * R) ** -0.5, 0.125),
        "far_ops": centred(splits[4], (CLS, R, R), (4 * R) ** -0.5, 0.1875),
        "list_seven": draw_list_seven(jax.random.fold_in(splits[10], 71), 0),
        "list_six": draw_list_six(jax.random.fold_in(splits[10], 71), 0),
        "list_five": draw_list_five(jax.random.fold_in(splits[10], 71), 0),
        "list_four": draw_list_four(jax.random.fold_in(splits[10], 71), 0),
        "list_three": draw_list_three(jax.random.fold_in(splits[10], 71), 0),
    }


def ascend(coef, octant_ops):
    rows, count = coef.shape
    grouped = coef.astype(jnp.float32).reshape(rows, count // 8, 8)
    parent = jnp.einsum('oij,jpo->ip', octant_ops.astype(jnp.float32), grouped)
    return parent.astype(jnp.bfloat16)


def descend(local, octant_ops):
    rows, count = local.shape
    rounded = lax.optimization_barrier(local.astype(jnp.bfloat16))
    spread = jnp.einsum('oji,jp->ipo', octant_ops.astype(jnp.float32), rounded.astype(jnp.float32))
    return spread.reshape(rows, count * 8)


def interact(coef, entries, far_ops):
    summed = jnp.zeros((coef.shape[0], entries.shape[1]), jnp.float32)
    for member in range(entries.shape[0]):
        present = entries[member] >= 0
        located = jnp.where(present, entries[member], 0).astype(jnp.int32)
        picked = jnp.take(coef, located, axis=1)
        picked = jnp.where(present[None, :], picked, jnp.zeros_like(picked))
        summed = summed + jnp.dot(far_ops[member], picked, preferred_element_type=jnp.float32)
    return summed


def reference(multipole, compress, expand, octant_ops, far_ops, list_seven, list_six, list_five, list_four, list_three):
    coef_seven = jnp.dot(compress, multipole, preferred_element_type=jnp.float32).astype(jnp.bfloat16)
    coef_six = ascend(coef_seven, octant_ops)
    coef_five = ascend(coef_six, octant_ops)
    coef_four = ascend(coef_five, octant_ops)
    coef_three = ascend(coef_four, octant_ops)
    far_seven = interact(coef_seven, list_seven, far_ops)
    far_six = interact(coef_six, list_six, far_ops) * 2.0
    far_five = interact(coef_five, list_five, far_ops) * 4.0
    far_four = interact(coef_four, list_four, far_ops) * 8.0
    far_three = interact(coef_three, list_three, far_ops) * 16.0
    local_four = far_four + descend(far_three, octant_ops)
    local_five = far_five + descend(local_four, octant_ops)
    local_six = far_six + descend(local_five, octant_ops)
    local_seven = far_seven + descend(local_six, octant_ops)
    return jnp.dot(expand, local_seven.astype(jnp.bfloat16), preferred_element_type=jnp.float32)
```

```python
import functools

import jax
import jax.numpy as jnp
from jax import lax
from jax.experimental import pallas as pl
from jax.experimental.pallas import tpu as pltpu
from jax.sharding import PartitionSpec as P

MESH = pl.DeviceIdType.MESH
F32 = jnp.float32
BF16 = jnp.bfloat16


def nt(a, b):
    return lax.dot_general(a, b, (((1,), (1,)), ((), ())), preferred_element_type=F32)


def nn(a, b):
    return jnp.dot(a, b, preferred_element_type=F32)


def iota(shape, axis):
    return lax.broadcasted_iota(jnp.int32, shape, axis)


def take_rows(ref, start, rows, stride=1):
    parts = [ref[h, pl.ds(start, rows, stride=stride), :] for h in range(ref.shape[0])]
    return jnp.concatenate(parts, axis=1)


def put_rows(ref, start, rows, value, stride=1):
    for h in range(ref.shape[0]):
        ref[h, pl.ds(start, rows, stride=stride), :] = value[:, h * 128 : (h + 1) * 128]


def onehot(column, width, start=0):
    rows = column.shape[0]
    return jnp.where(iota((rows, width), 1) + start == column, 1.0, 0.0).astype(BF16)


def kernel(
    sizes,
    mult_h,
    comp_h,
    expd_h,
    octs_h,
    fars_h,
    l7_h,
    l6_h,
    l5_h,
    l4_h,
    l3_h,
    out_h,
    mult,
    comp,
    expd,
    octs,
    fars,
    l7,
    l6,
    l5,
    l4,
    l3,
    c7f,
    c6f,
    c4f,
    halo,
    small,
    every,
    own_pick,
    acc,
    d6,
    d7,
    outv,
    load_sem,
    out_sem,
    send_sem,
    recv_sem,
    all_send,
    all_recv,
):
    axes, counts, classes, nb4, nb3 = sizes
    n = counts[0] * counts[1]
    b7 = c7f.shape[1]
    b6 = b7 // 8
    b5 = b6 // 8
    per4 = 8 // b5
    block = b6 + 16
    me = lax.axis_index(axes[0]) * counts[1] + lax.axis_index(axes[1])

    def place(peer):
        return (peer // counts[1], peer % counts[1])

    loads = [
        pltpu.make_async_copy(src, dst, load_sem.at[k])
        for k, (src, dst) in enumerate(
            [
                (comp_h, comp),
                (mult_h, mult),
                (octs_h, octs),
                (l7_h, l7),
                (l6_h, l6),
                (l5_h, l5),
                (l4_h, l4),
                (l3_h, l3),
                (fars_h, fars),
                (expd_h, expd),
            ]
        )
    ]
    for load in loads:
        load.start()

    barrier = pltpu.get_barrier_semaphore()

    def greet(k, carry):
        pl.semaphore_signal(
            barrier, inc=1, device_id=place(lax.rem(me + k, n)), device_id_type=MESH
        )
        return carry

    lax.fori_loop(1, n, greet, 0)
    c6f[...] = jnp.zeros_like(c6f)
    c4f[...] = jnp.zeros_like(c4f)

    loads[0].wait()
    loads[1].wait()
    seven = nn(comp[...], mult[...]).astype(BF16).astype(F32).T
    put_rows(c7f, 0, b7, seven)
    halo[b7 : 2 * b7, :] = seven.astype(BF16)

    pl.semaphore_wait(barrier, n - 1)
    right = place(lax.rem(me + 1, n))
    left = place(lax.rem(me + n - 1, n))

    def halo_copy(ref, rows, slot, peer, index):
        return pltpu.make_async_remote_copy(
            src_ref=ref.at[pl.ds(rows, rows), :],
            dst_ref=ref.at[pl.ds(slot * rows, rows), :],
            send_sem=send_sem.at[index],
            recv_sem=recv_sem.at[index],
            device_id=peer,
            device_id_type=MESH,
        )

    halo_sends = [
        halo_copy(halo, b7, 0, right, 0),
        halo_copy(halo, b7, 2, left, 1),
    ]
    for copy in halo_sends:
        copy.start()

    loads[2].wait()
    total = jnp.zeros((b6, octs.shape[1]), F32)
    for o in range(8):
        total = total + nt(take_rows(c7f, o, b6, 8).astype(BF16), octs[o])
    six = total.astype(BF16)
    put_rows(c6f, 0, b6, six.astype(F32))
    total = jnp.zeros((16, octs.shape[1]), F32)
    for o in range(8):
        total = total + nt(take_rows(c6f, o, 16, 8).astype(BF16), octs[o])
    five = total.astype(BF16)
    small[block : block + b6, :] = six
    small[block + b6 : 2 * block, :] = five
    fivef = five.astype(F32)
    half = octs.shape[1] // 2
    tile = jnp.concatenate([fivef[0:b5, :half], fivef[0:b5, half:]], axis=0)
    mine = pl.ds(pl.multiple_of(me * 8, 8), 8)
    every[mine, :] = tile

    small_sends = [
        halo_copy(small, block, 0, right, 2),
        halo_copy(small, block, 2, left, 3),
    ]

    def spread(k, carry):
        pltpu.make_async_remote_copy(
            src_ref=every.at[mine, :],
            dst_ref=every.at[mine, :],
            send_sem=all_send,
            recv_sem=all_recv,
            device_id=place(lax.rem(me + k, n)),
            device_id_type=MESH,
        ).start()
        return carry

    lax.fori_loop(1, n, spread, 0)
    for copy in small_sends:
        copy.start()

    for k in range(3, 8):
        loads[k].wait()
    e7 = l7[...]
    p7 = jnp.where(e7 >= 0, e7 - (me * b7 - b7), -1).astype(F32).T.astype(jnp.int32)
    e6 = l6[...]
    p6 = e6 - (me * b6 - b6)
    p6 = p6 + jnp.where(p6 >= b6, block - b6, 0) + jnp.where(p6 >= 2 * b6, block - b6, 0)
    p6 = jnp.where(e6 >= 0, p6, -1).astype(F32)
    e5 = l5[...]
    p5 = e5 - (me * b5 - b5)
    p5 = p5 + b6 + jnp.where(p5 >= b5, block - b5, 0) + jnp.where(p5 >= 2 * b5, block - b5, 0)
    p5 = jnp.where(e5 >= 0, p5, -1).astype(F32)

    def column(row, rows):
        shape = (rows, row.shape[1])
        spread_row = jnp.where(iota(shape, 0) == iota(shape, 1), row, -1.0)
        return jnp.max(spread_row, axis=1, keepdims=True)

    for c in range(classes):
        own_pick[c] = nn(onehot(p7[:, c : c + 1], b7, b7), halo[b7 : 2 * b7, :]).astype(BF16)

    for copy in halo_sends + small_sends:
        copy.wait_recv()
    loads[8].wait()
    for c in range(classes):
        col = p7[:, c : c + 1]
        picked = own_pick[c].astype(F32)
        picked = picked + nn(onehot(col, b7, 0), halo[0:b7, :])
        picked = picked + nn(onehot(col, b7, 2 * b7), halo[2 * b7 : 3 * b7, :])
        cols = jnp.concatenate(
            [column(p6[c : c + 1, :], b6), column(p5[c : c + 1, :], 16)], axis=0
        ).astype(jnp.int32)
        lesser = nn(onehot(cols, 3 * block), small[...])
        both = jnp.concatenate([picked, lesser], axis=0).astype(BF16)
        if c == 0:
            acc[...] = nt(both, fars[c])
        else:
            acc[...] += nt(both, fars[c])

    rest = every.at[pl.ds(0, (n - 1) * 8), :]
    pltpu.make_async_copy(rest, rest, all_recv).wait()
    total = jnp.zeros((nb4, octs.shape[1]), F32)
    for o in range(8):
        at = (o // b5) * 8 + o % b5
        low = every[pl.ds(at, nb4, stride=8 * per4), :]
        high = every[pl.ds(at + b5, nb4, stride=8 * per4), :]
        total = total + nt(jnp.concatenate([low, high], axis=1).astype(BF16), octs[o])
    put_rows(c4f, 0, nb4, total.astype(BF16).astype(F32))
    rows3 = c4f.shape[1] // 8
    total = jnp.zeros((rows3, octs.shape[1]), F32)
    for o in range(8):
        total = total + nt(take_rows(c4f, o, rows3, 8).astype(BF16), octs[o])
    three = total.astype(BF16)
    t4 = me // per4
    t3 = t4 // 8

    def picked_one(entries, target, coef):
        lanes = iota(entries.shape, 1)
        chosen = jnp.where(lanes == target, entries, -1).astype(F32)
        col = jnp.max(chosen, axis=1, keepdims=True).astype(jnp.int32)
        return nn(onehot(col, coef.shape[0]), coef.astype(BF16))

    upper = jnp.concatenate(
        [picked_one(l4[...], t4, take_rows(c4f, 0, 8 * rows3)), picked_one(l3[...], t3, three)], axis=0
    )
    row = iota(upper.shape, 0) % classes
    total = jnp.zeros(upper.shape, F32)
    for c in range(classes):
        total = total + nt(jnp.where(row == c, upper, 0.0).astype(BF16), fars[c])
    far4 = 8.0 * jnp.sum(total[:classes], axis=0, keepdims=True)
    far3 = 16.0 * jnp.sum(total[classes:], axis=0, keepdims=True)

    wide = (16, octs.shape[1])
    down = nn(jnp.broadcast_to(far3, wide).astype(BF16), octs[t4 % 8])
    local4 = jnp.broadcast_to(far4 + down[0:1, :], wide)
    local5 = 4.0 * acc[b7 + b6 : b7 + block, :]
    first = (me % per4) * b5
    for k in range(b5):
        local5 = local5 + nn(
            jnp.where(iota(wide, 0) == k, local4, 0.0).astype(BF16), octs[first + k]
        )
    local5 = local5.astype(BF16)
    for o in range(8):
        put_rows(d6, o, 8, nn(local5, octs[o])[0:8, :], 8)
    local6 = (2.0 * acc[b7 : b7 + b6, :] + take_rows(d6, 0, b6)).astype(BF16)
    for o in range(8):
        put_rows(d7, o, b6, nn(local6, octs[o]), 8)
    local7 = (acc[0:b7, :] + take_rows(d7, 0, b7)).astype(BF16)

    loads[9].wait()
    surface = expd.shape[0]
    step = 304
    stores = []
    for k, start in enumerate(range(0, surface, step)):
        stop = min(start + step, surface)
        outv[start:stop, :] = nt(expd[start:stop, :], local7)
        store = pltpu.make_async_copy(
            outv.at[pl.ds(start, stop - start), :],
            out_h.at[pl.ds(start, stop - start), :],
            out_sem.at[k],
        )
        store.start()
        stores.append(store)
    for copy in halo_sends + small_sends:
        copy.wait_send()
    pltpu.make_async_copy(rest, rest, all_send).wait()
    for store in stores:
        store.wait()


def on_device(axes, counts, *args):
    mult, comp, expd, octs, fars, l7, l6, l5, l4, l3 = args
    n = counts[0] * counts[1]
    b7, b6, b5 = l7.shape[1], l6.shape[1], l5.shape[1]
    nb4, nb3 = l4.shape[1], l3.shape[1]
    classes, r = fars.shape[0], fars.shape[1]
    if b6 * 8 != b7 or b5 * 8 != b6 or b5 != 4:
        raise ValueError("unsupported sizes")
    block = b6 + 16
    rows3 = max(16, nb3)
    scratch = [pltpu.VMEM(a.shape, a.dtype) for a in args]
    scratch += [
        pltpu.VMEM((r // 128, b7, 128), F32),
        pltpu.VMEM((r // 128, 128, 128), F32),
        pltpu.VMEM((r // 128, rows3 * 8, 128), F32),
        pltpu.VMEM((3 * b7, r), BF16),
        pltpu.VMEM((3 * block, r), BF16),
        pltpu.VMEM((n * 8, r // 2), F32),
        pltpu.VMEM((classes, b7, r), BF16),
        pltpu.VMEM((b7 + block, r), F32),
        pltpu.VMEM((r // 128, 64, 128), F32),
        pltpu.VMEM((r // 128, b7, 128), F32),
        pltpu.VMEM((expd.shape[0], b7), F32),
        pltpu.SemaphoreType.DMA((10,)),
        pltpu.SemaphoreType.DMA((3,)),
        pltpu.SemaphoreType.DMA((4,)),
        pltpu.SemaphoreType.DMA((4,)),
        pltpu.SemaphoreType.DMA,
        pltpu.SemaphoreType.DMA,
    ]
    return pl.pallas_call(
        functools.partial(kernel, (axes, counts, classes, nb4, nb3)),
        out_shape=jax.ShapeDtypeStruct((expd.shape[0], b7), F32),
        in_specs=[pl.BlockSpec(memory_space=pl.ANY)] * len(args),
        out_specs=pl.BlockSpec(memory_space=pl.ANY),
        scratch_shapes=scratch,
        compiler_params=pltpu.CompilerParams(
            collective_id=0, has_side_effects=True, vmem_limit_bytes=50 * 1024 * 1024
        ),
    )(*args)


def solution(mesh):
    axes = tuple(mesh.axis_names)
    counts = tuple(mesh.shape[a] for a in axes)
    cut = P(None, axes)
    return jax.shard_map(
        functools.partial(on_device, axes, counts),
        mesh=mesh,
        in_specs=(cut, P(), P(), P(), P(), cut, cut, cut, P(), P()),
        out_specs=cut,
        check_vma=False,
    )
```

```python
import functools

import jax
import jax.numpy as jnp
from jax import lax
from jax.experimental import pallas as pl
from jax.experimental.pallas import tpu as pltpu
from jax.sharding import PartitionSpec as P

MESH = pl.DeviceIdType.MESH
F32 = jnp.float32
BF16 = jnp.bfloat16


def nt(a, b):
    return lax.dot_general(a, b, (((1,), (1,)), ((), ())), preferred_element_type=F32)


def tn(a, b):
    return lax.dot_general(a, b, (((0,), (0,)), ((), ())), preferred_element_type=F32)


def nn(a, b):
    return jnp.dot(a, b, preferred_element_type=F32)


def iota(shape, axis):
    return lax.broadcasted_iota(jnp.int32, shape, axis)


def take_rows(ref, start, rows, stride=1):
    parts = [ref[h, pl.ds(start, rows, stride=stride), :] for h in range(ref.shape[0])]
    return jnp.concatenate(parts, axis=1)


def put_rows(ref, start, rows, value, stride=1):
    for h in range(ref.shape[0]):
        ref[h, pl.ds(start, rows, stride=stride), :] = value[:, h * 128 : (h + 1) * 128]


def onehot(column, width, start=0):
    rows = column.shape[0]
    return jnp.where(iota((rows, width), 1) + start == column, 1.0, 0.0).astype(BF16)


def column(row, rows):
    shape = (rows, row.shape[1])
    spread_row = jnp.where(iota(shape, 0) == iota(shape, 1), row, -1.0)
    return jnp.max(spread_row, axis=1, keepdims=True)


def kernel(
    sizes,
    mult_h,
    comp_h,
    expd_h,
    octs_h,
    fars_h,
    l7_h,
    l6_h,
    l5_h,
    l4_h,
    l3_h,
    outv,
    mult,
    comp,
    expd,
    octs,
    fars,
    l7,
    l6,
    l5,
    l4,
    l3,
    c7f,
    c6f,
    c4f,
    own,
    halo,
    small,
    every,
    own_pick,
    hot,
    hot_small,
    acc,
    d6,
    d7,
    load_sem,
    send_sem,
    recv_sem,
    all_send,
    all_recv,
):
    axes, counts, classes, nb4, nb3 = sizes
    n = counts[0] * counts[1]
    b7 = c7f.shape[1]
    b6 = b7 // 8
    b5 = b6 // 8
    per4 = 8 // b5
    block = b6 + 16
    me = lax.axis_index(axes[0]) * counts[1] + lax.axis_index(axes[1])

    def place(peer):
        return (peer // counts[1], peer % counts[1])

    loads = [
        pltpu.make_async_copy(src, dst, load_sem.at[k])
        for k, (src, dst) in enumerate(
            [
                (comp_h, comp),
                (mult_h, mult),
                (octs_h, octs),
                (l7_h, l7),
                (l6_h, l6),
                (l5_h, l5),
                (l4_h, l4),
                (l3_h, l3),
                (fars_h, fars),
                (expd_h, expd),
            ]
        )
    ]
    for load in loads[:8]:
        load.start()

    barrier = pltpu.get_barrier_semaphore()

    def greet(k, carry):
        pl.semaphore_signal(
            barrier, inc=1, device_id=place(lax.rem(me + k, n)), device_id_type=MESH
        )
        return carry

    lax.fori_loop(1, n, greet, 0)
    c6f[...] = jnp.zeros_like(c6f)
    c4f[...] = jnp.zeros_like(c4f)

    loads[0].wait()
    loads[1].wait()
    loads[8].start()
    loads[9].start()
    seven = tn(mult[...], comp[...]).astype(BF16)
    own[...] = seven
    put_rows(c7f, 0, b7, seven.astype(F32))

    pl.semaphore_wait(barrier, n - 1)
    right = place(lax.rem(me + 1, n))
    left = place(lax.rem(me + n - 1, n))

    def halo_copy(src, ref, rows, slot, peer, index):
        return pltpu.make_async_remote_copy(
            src_ref=src,
            dst_ref=ref.at[pl.ds(slot * rows, rows), :],
            send_sem=send_sem.at[index],
            recv_sem=recv_sem.at[index],
            device_id=peer,
            device_id_type=MESH,
        )

    halo_sends = [
        halo_copy(own, halo, b7, 0, right, 0),
        halo_copy(own, halo, b7, 1, left, 1),
    ]
    for copy in halo_sends:
        copy.start()

    loads[2].wait()
    total = jnp.zeros((b6, octs.shape[1]), F32)
    for o in range(8):
        total = total + nt(take_rows(c7f, o, b6, 8).astype(BF16), octs[o])
    six = total.astype(BF16)
    put_rows(c6f, 0, b6, six.astype(F32))
    total = jnp.zeros((16, octs.shape[1]), F32)
    for o in range(8):
        total = total + nt(take_rows(c6f, o, 16, 8).astype(BF16), octs[o])
    five = total.astype(BF16)
    small[block : block + b6, :] = six
    small[block + b6 : 2 * block, :] = five
    fivef = five.astype(F32)
    half = octs.shape[1] // 2
    tile = jnp.concatenate([fivef[0:b5, :half], fivef[0:b5, half:]], axis=0)
    mine = pl.ds(pl.multiple_of(me * 8, 8), 8)
    every[mine, :] = tile

    small_sends = [
        halo_copy(small.at[pl.ds(block, block), :], small, block, 0, right, 2),
        halo_copy(small.at[pl.ds(block, block), :], small, block, 2, left, 3),
    ]

    def spread(k, carry):
        pltpu.make_async_remote_copy(
            src_ref=every.at[mine, :],
            dst_ref=every.at[mine, :],
            send_sem=all_send,
            recv_sem=all_recv,
            device_id=place(lax.rem(me + k, n)),
            device_id_type=MESH,
        ).start()
        return carry

    lax.fori_loop(1, n, spread, 0)
    for copy in small_sends:
        copy.start()

    for k in range(3, 8):
        loads[k].wait()
    e7 = l7[...]
    p7 = jnp.where(e7 >= 0, e7 - (me * b7 - b7), -1).astype(F32).T.astype(jnp.int32)
    e6 = l6[...]
    p6 = e6 - (me * b6 - b6)
    p6 = p6 + jnp.where(p6 >= b6, block - b6, 0) + jnp.where(p6 >= 2 * b6, block - b6, 0)
    p6 = jnp.where(e6 >= 0, p6, -1).astype(F32)
    e5 = l5[...]
    p5 = e5 - (me * b5 - b5)
    p5 = p5 + b6 + jnp.where(p5 >= b5, block - b5, 0) + jnp.where(p5 >= 2 * b5, block - b5, 0)
    p5 = jnp.where(e5 >= 0, p5, -1)
    p5 = jnp.concatenate([p5, jnp.full((16 - b5, classes), -1, jnp.int32)], axis=0)

    for c in range(classes):
        col = p7[:, c : c + 1]
        own_pick[c] = nn(onehot(col, b7, b7), own[...]).astype(BF16)
        hot[c, :, 0:b7] = onehot(col, b7, 0)
        hot[c, :, b7 : 2 * b7] = onehot(col, b7, 2 * b7)
        cols = jnp.concatenate(
            [column(p6[c : c + 1, :], b6).astype(jnp.int32), p5[:, c : c + 1]], axis=0
        )
        hot_small[c] = onehot(cols, 3 * block)

    loads[8].wait()
    rest = every.at[pl.ds(0, (n - 1) * 8), :]
    pltpu.make_async_copy(rest, rest, all_recv).wait()
    total = jnp.zeros((nb4, octs.shape[1]), F32)
    for o in range(8):
        at = (o // b5) * 8 + o % b5
        low = every[pl.ds(at, nb4, stride=8 * per4), :]
        high = every[pl.ds(at + b5, nb4, stride=8 * per4), :]
        total = total + nt(jnp.concatenate([low, high], axis=1).astype(BF16), octs[o])
    put_rows(c4f, 0, nb4, total.astype(BF16).astype(F32))
    rows3 = c4f.shape[1] // 8
    total = jnp.zeros((rows3, octs.shape[1]), F32)
    for o in range(8):
        total = total + nt(take_rows(c4f, o, rows3, 8).astype(BF16), octs[o])
    three = total.astype(BF16)
    t4 = me // per4
    t3 = t4 // 8

    e4 = l4[...]
    chosen4 = jnp.where(iota(e4.shape, 1) == t4, e4, -1).astype(F32)
    chosen4 = jnp.max(chosen4, axis=1, keepdims=True).astype(jnp.int32)
    e3 = l3[...]
    chosen3 = jnp.where(iota(e3.shape, 0) == t3, e3, -1).astype(F32)
    chosen3 = column(jnp.max(chosen3, axis=0, keepdims=True), classes).astype(jnp.int32)
    four = take_rows(c4f, 0, 8 * rows3).astype(BF16)
    upper = jnp.concatenate(
        [nn(onehot(chosen4, 8 * rows3), four), nn(onehot(chosen3, rows3), three)], axis=0
    )
    row = iota(upper.shape, 0) % classes
    total = jnp.zeros(upper.shape, F32)
    for c in range(classes):
        total = total + nt(jnp.where(row == c, upper, 0.0).astype(BF16), fars[c])
    far4 = 8.0 * jnp.sum(total[:classes], axis=0, keepdims=True)
    far3 = 16.0 * jnp.sum(total[classes:], axis=0, keepdims=True)

    wide = (16, octs.shape[1])
    down = nn(jnp.broadcast_to(far3, wide).astype(BF16), octs[t4 % 8])
    local4 = jnp.broadcast_to(far4 + down[0:1, :], wide)
    local5 = jnp.zeros(wide, F32)
    first = (me % per4) * b5
    for k in range(b5):
        local5 = local5 + nn(
            jnp.where(iota(wide, 0) == k, local4, 0.0).astype(BF16), octs[first + k]
        )
    for copy in halo_sends + small_sends:
        copy.wait_recv()
    for c in range(classes):
        picked = nn(hot[c], halo[...]) + own_pick[c].astype(F32)
        lesser = nn(hot_small[c], small[...])
        both = jnp.concatenate([picked, lesser], axis=0).astype(BF16)
        if c == 0:
            acc[...] = nt(both, fars[c])
        else:
            acc[...] += nt(both, fars[c])

    local5 = (4.0 * acc[b7 + b6 : b7 + block, :] + local5).astype(BF16)
    for o in range(8):
        put_rows(d6, o, 8, nn(local5, octs[o])[0:8, :], 8)
    local6 = (2.0 * acc[b7 : b7 + b6, :] + take_rows(d6, 0, b6)).astype(BF16)
    for o in range(8):
        put_rows(d7, o, b6, nn(local6, octs[o]), 8)
    local7 = (acc[0:b7, :] + take_rows(d7, 0, b7)).astype(BF16)

    loads[9].wait()
    surface = expd.shape[0]
    step = 304
    for start in range(0, surface, step):
        stop = min(start + step, surface)
        outv[start:stop, :] = nt(expd[start:stop, :], local7)
    for copy in halo_sends + small_sends:
        copy.wait_send()
    pltpu.make_async_copy(rest, rest, all_send).wait()


def on_device(axes, counts, *args):
    mult, comp, expd, octs, fars, l7, l6, l5, l4, l3 = args
    args = (mult, comp.T, expd, octs, fars, l7, l6, l5.T, l4, l3.T)
    n = counts[0] * counts[1]
    b7, b6, b5 = l7.shape[1], l6.shape[1], l5.shape[1]
    nb4, nb3 = l4.shape[1], l3.shape[1]
    classes, r = fars.shape[0], fars.shape[1]
    if b6 * 8 != b7 or b5 * 8 != b6 or b5 != 4:
        raise ValueError("unsupported sizes")
    block = b6 + 16
    rows3 = max(16, nb3)
    scratch = [pltpu.VMEM(a.shape, a.dtype) for a in args]
    scratch += [
        pltpu.VMEM((r // 128, b7, 128), F32),
        pltpu.VMEM((r // 128, 128, 128), F32),
        pltpu.VMEM((r // 128, rows3 * 8, 128), F32),
        pltpu.VMEM((b7, r), BF16),
        pltpu.VMEM((2 * b7, r), BF16),
        pltpu.VMEM((3 * block, r), BF16),
        pltpu.VMEM((n * 8, r // 2), F32),
        pltpu.VMEM((classes, b7, r), BF16),
        pltpu.VMEM((classes, b7, 2 * b7), BF16),
        pltpu.VMEM((classes, block, 3 * block), BF16),
        pltpu.VMEM((b7 + block, r), F32),
        pltpu.VMEM((r // 128, 64, 128), F32),
        pltpu.VMEM((r // 128, b7, 128), F32),
        pltpu.SemaphoreType.DMA((10,)),
        pltpu.SemaphoreType.DMA((4,)),
        pltpu.SemaphoreType.DMA((4,)),
        pltpu.SemaphoreType.DMA,
        pltpu.SemaphoreType.DMA,
    ]
    return pl.pallas_call(
        functools.partial(kernel, (axes, counts, classes, nb4, nb3)),
        out_shape=jax.ShapeDtypeStruct((expd.shape[0], b7), F32),
        in_specs=[pl.BlockSpec(memory_space=pltpu.HBM)] * len(args),
        out_specs=pl.BlockSpec(memory_space=pltpu.VMEM),
        scratch_shapes=scratch,
        compiler_params=pltpu.CompilerParams(
            collective_id=0, has_side_effects=True, vmem_limit_bytes=60 * 1024 * 1024
        ),
    )(*args)


def solution(mesh):
    axes = tuple(mesh.axis_names)
    counts = tuple(mesh.shape[a] for a in axes)
    cut = P(None, axes)
    return jax.shard_map(
        functools.partial(on_device, axes, counts),
        mesh=mesh,
        in_specs=(cut, P(), P(), P(), P(), cut, cut, cut, P(), P()),
        out_specs=cut,
        check_vma=False,
    )
```

```python
import functools

import jax
import jax.numpy as jnp
from jax import lax
from jax.experimental import pallas as pl
from jax.experimental.pallas import tpu as pltpu
from jax.sharding import PartitionSpec as P

MESH = pl.DeviceIdType.MESH
F32 = jnp.float32
BF16 = jnp.bfloat16


def nt(a, b):
    return lax.dot_general(a, b, (((1,), (1,)), ((), ())), preferred_element_type=F32)


def tn(a, b):
    return lax.dot_general(a, b, (((0,), (0,)), ((), ())), preferred_element_type=F32)


def nn(a, b):
    return jnp.dot(a, b, preferred_element_type=F32)


def iota(shape, axis):
    return lax.broadcasted_iota(jnp.int32, shape, axis)


def take_rows(ref, start, rows, stride=1):
    parts = [ref[h, pl.ds(start, rows, stride=stride), :] for h in range(ref.shape[0])]
    return jnp.concatenate(parts, axis=1)


def put_rows(ref, start, rows, value, stride=1):
    for h in range(ref.shape[0]):
        ref[h, pl.ds(start, rows, stride=stride), :] = value[:, h * 128 : (h + 1) * 128]


def onehot(column, width, start=0):
    rows = column.shape[0]
    return jnp.where(iota((rows, width), 1) + start == column, 1.0, 0.0).astype(BF16)


def column(row, rows):
    shape = (rows, row.shape[1])
    spread_row = jnp.where(iota(shape, 0) == iota(shape, 1), row, -1.0)
    return jnp.max(spread_row, axis=1, keepdims=True)


def kernel(
    sizes,
    mult_h,
    comp_h,
    expd_h,
    octs_h,
    fars_h,
    l7_h,
    l6_h,
    l5_h,
    l4_h,
    l3_h,
    outv,
    mult,
    comp,
    expd,
    octs,
    fars,
    l7,
    l6,
    l5,
    l4,
    l3,
    c7f,
    c6f,
    c4f,
    own,
    halo,
    small,
    every,
    own_pick,
    hot,
    hot_small,
    acc,
    d6,
    d7,
    load_sem,
    send_sem,
    recv_sem,
    all_send,
    all_recv,
):
    axes, counts, classes, nb4, nb3 = sizes
    n = counts[0] * counts[1]
    b7 = c7f.shape[1]
    b6 = b7 // 8
    b5 = b6 // 8
    per4 = 8 // b5
    block = b6 + 16
    me = lax.axis_index(axes[0]) * counts[1] + lax.axis_index(axes[1])

    def place(peer):
        return (peer // counts[1], peer % counts[1])

    loads = [
        pltpu.make_async_copy(src, dst, load_sem.at[k])
        for k, (src, dst) in enumerate(
            [
                (comp_h, comp),
                (mult_h, mult),
                (octs_h, octs),
                (l7_h, l7),
                (l6_h, l6),
                (l5_h, l5),
                (l4_h, l4),
                (l3_h, l3),
                (fars_h, fars),
                (expd_h, expd),
            ]
        )
    ]
    for load in loads[:8]:
        load.start()

    barrier = pltpu.get_barrier_semaphore()

    def greet(k, carry):
        pl.semaphore_signal(
            barrier, inc=1, device_id=place(lax.rem(me + k, n)), device_id_type=MESH
        )
        return carry

    lax.fori_loop(1, n, greet, 0)
    c6f[...] = jnp.zeros_like(c6f)
    c4f[...] = jnp.zeros_like(c4f)
    rows3 = c4f.shape[1] // 8
    base4 = 3 * block
    base3 = base4 + nb4
    depth = small.shape[0]
    t4 = me // per4
    t3 = t4 // 8

    loads[0].wait()
    loads[1].wait()
    loads[8].start()
    loads[9].start()
    seven = tn(mult[...], comp[...]).astype(BF16)
    own[...] = seven
    put_rows(c7f, 0, b7, seven.astype(F32))

    pl.semaphore_wait(barrier, n - 1)
    right = place(lax.rem(me + 1, n))
    left = place(lax.rem(me + n - 1, n))

    def halo_copy(src, ref, rows, slot, peer, index):
        return pltpu.make_async_remote_copy(
            src_ref=src,
            dst_ref=ref.at[pl.ds(slot * rows, rows), :],
            send_sem=send_sem.at[index],
            recv_sem=recv_sem.at[index],
            device_id=peer,
            device_id_type=MESH,
        )

    halo_sends = [
        halo_copy(own, halo, b7, 0, right, 0),
        halo_copy(own, halo, b7, 1, left, 1),
    ]
    for copy in halo_sends:
        copy.start()

    loads[2].wait()
    total = jnp.zeros((b6, octs.shape[1]), F32)
    for o in range(8):
        total = total + nt(take_rows(c7f, o, b6, 8).astype(BF16), octs[o])
    six = total.astype(BF16)
    put_rows(c6f, 0, b6, six.astype(F32))
    total = jnp.zeros((16, octs.shape[1]), F32)
    for o in range(8):
        total = total + nt(take_rows(c6f, o, 16, 8).astype(BF16), octs[o])
    five = total.astype(BF16)
    small[block : block + b6, :] = six
    small[block + b6 : 2 * block, :] = five
    fivef = five.astype(F32)
    half = octs.shape[1] // 2
    tile = jnp.concatenate([fivef[0:b5, :half], fivef[0:b5, half:]], axis=0)
    mine = pl.ds(pl.multiple_of(me * 8, 8), 8)
    every[mine, :] = tile

    small_sends = [
        halo_copy(small.at[pl.ds(block, block), :], small, block, 0, right, 2),
        halo_copy(small.at[pl.ds(block, block), :], small, block, 2, left, 3),
    ]

    def spread(k, carry):
        pltpu.make_async_remote_copy(
            src_ref=every.at[mine, :],
            dst_ref=every.at[mine, :],
            send_sem=all_send,
            recv_sem=all_recv,
            device_id=place(lax.rem(me + k, n)),
            device_id_type=MESH,
        ).start()
        return carry

    lax.fori_loop(1, n, spread, 0)
    for copy in small_sends:
        copy.start()

    for k in range(3, 8):
        loads[k].wait()
    e7 = l7[...]
    p7 = jnp.where(e7 >= 0, e7 - (me * b7 - b7), -1).astype(F32).T.astype(jnp.int32)
    e6 = l6[...]
    p6 = e6 - (me * b6 - b6)
    p6 = p6 + jnp.where(p6 >= b6, block - b6, 0) + jnp.where(p6 >= 2 * b6, block - b6, 0)
    p6 = jnp.where(e6 >= 0, p6, -1).astype(F32)
    e5 = l5[...]
    p5 = e5 - (me * b5 - b5)
    p5 = p5 + b6 + jnp.where(p5 >= b5, block - b5, 0) + jnp.where(p5 >= 2 * b5, block - b5, 0)
    p5 = jnp.where(e5 >= 0, p5, -1)
    p5 = jnp.concatenate([p5, jnp.full((16 - b5, classes), -1, jnp.int32)], axis=0)

    e4 = l4[...]
    p4 = jnp.where(iota(e4.shape, 1) == t4, e4, -1).astype(F32)
    p4 = jnp.max(p4, axis=1, keepdims=True).astype(jnp.int32)
    p4 = jnp.where(p4 >= 0, p4 + base4, -1)
    e3 = l3[...]
    p3 = jnp.where(iota(e3.shape, 0) == t3, e3, -1).astype(F32)
    p3 = column(jnp.max(p3, axis=0, keepdims=True), classes).astype(jnp.int32)
    p3 = jnp.where(p3 >= 0, p3 + base3, -1)
    row = iota((16, 1), 0)

    for c in range(classes):
        col = p7[:, c : c + 1]
        own_pick[c] = nn(onehot(col, b7, b7), own[...]).astype(BF16)
        hot[c, :, 0:b7] = onehot(col, b7, 0)
        hot[c, :, b7 : 2 * b7] = onehot(col, b7, 2 * b7)
        tail = jnp.where(row == b5, p4[c : c + 1, :], p5[:, c : c + 1])
        tail = jnp.where(row == b5 + 1, p3[c : c + 1, :], tail)
        cols = jnp.concatenate([column(p6[c : c + 1, :], b6).astype(jnp.int32), tail], axis=0)
        hot_small[c] = onehot(cols, depth)

    loads[8].wait()
    rest = every.at[pl.ds(0, (n - 1) * 8), :]
    pltpu.make_async_copy(rest, rest, all_recv).wait()
    for copy in halo_sends + small_sends:
        copy.wait_recv()

    def coarser():
        total = jnp.zeros((nb4, octs.shape[1]), F32)
        for o in range(8):
            at = (o // b5) * 8 + o % b5
            low = every[pl.ds(at, nb4, stride=8 * per4), :]
            high = every[pl.ds(at + b5, nb4, stride=8 * per4), :]
            total = total + nt(jnp.concatenate([low, high], axis=1).astype(BF16), octs[o])
            if o % 4 == 3:
                yield
        four = total.astype(BF16)
        put_rows(c4f, 0, nb4, four.astype(F32))
        small[base4 : base4 + nb4, :] = four
        total = jnp.zeros((rows3, octs.shape[1]), F32)
        for o in range(8):
            total = total + nt(take_rows(c4f, o, rows3, 8).astype(BF16), octs[o])
            if o % 4 == 3:
                yield
        small[base3 : base3 + rows3, :] = total.astype(BF16)
        far = jnp.zeros((block, octs.shape[1]), F32)
        for c in range(classes):
            lesser = nn(hot_small[c], small[...]).astype(BF16)
            far = far + nt(lesser, fars[c])
            if c % 4 == 3:
                yield
        far6, far5 = 2.0 * far[0:b6, :], 4.0 * far[b6:block, :]
        far4 = 8.0 * far[b6 + b5 : b6 + b5 + 1, :]
        far3 = 16.0 * far[b6 + b5 + 1 : b6 + b5 + 2, :]
        wide = (16, octs.shape[1])
        down = nn(jnp.broadcast_to(far3, wide).astype(BF16), octs[t4 % 8])
        local4 = jnp.broadcast_to(far4 + down[0:1, :], wide)
        yield
        local5 = far5
        first = (me % per4) * b5
        for k in range(b5):
            local5 = local5 + nn(
                jnp.where(iota(wide, 0) == k, local4, 0.0).astype(BF16), octs[first + k]
            )
        local5 = local5.astype(BF16)
        yield
        for o in range(8):
            put_rows(d6, o, 8, nn(local5, octs[o])[0:8, :], 8)
        local6 = (far6 + take_rows(d6, 0, b6)).astype(BF16)
        yield
        for o in range(8):
            put_rows(d7, o, b6, nn(local6, octs[o]), 8)
            if o % 4 == 3:
                yield

    chain = coarser()
    next(chain, None)
    for c in range(classes):
        next(chain, None)
        picked = nn(hot[c], halo[...]) + own_pick[c].astype(F32)
        if c == 0:
            acc[...] = nt(picked.astype(BF16), fars[c])
        else:
            acc[...] += nt(picked.astype(BF16), fars[c])
    for _ in chain:
        pass
    local7 = (acc[...] + take_rows(d7, 0, b7)).astype(BF16)

    loads[9].wait()
    surface = expd.shape[0]
    step = 304
    for start in range(0, surface, step):
        stop = min(start + step, surface)
        outv[start:stop, :] = nt(expd[start:stop, :], local7)
    for copy in halo_sends + small_sends:
        copy.wait_send()
    pltpu.make_async_copy(rest, rest, all_send).wait()


def on_device(axes, counts, *args):
    mult, comp, expd, octs, fars, l7, l6, l5, l4, l3 = args
    args = (mult, comp.T, expd, octs, fars, l7, l6, l5.T, l4, l3.T)
    n = counts[0] * counts[1]
    b7, b6, b5 = l7.shape[1], l6.shape[1], l5.shape[1]
    nb4, nb3 = l4.shape[1], l3.shape[1]
    classes, r = fars.shape[0], fars.shape[1]
    if b6 * 8 != b7 or b5 * 8 != b6 or b5 != 4 or nb4 % 16:
        raise ValueError("unsupported sizes")
    block = b6 + 16
    rows3 = max(16, nb3)
    depth = 3 * block + nb4 + rows3
    scratch = [pltpu.VMEM(a.shape, a.dtype) for a in args]
    scratch += [
        pltpu.VMEM((r // 128, b7, 128), F32),
        pltpu.VMEM((r // 128, 128, 128), F32),
        pltpu.VMEM((r // 128, rows3 * 8, 128), F32),
        pltpu.VMEM((b7, r), BF16),
        pltpu.VMEM((2 * b7, r), BF16),
        pltpu.VMEM((depth, r), BF16),
        pltpu.VMEM((n * 8, r // 2), F32),
        pltpu.VMEM((classes, b7, r), BF16),
        pltpu.VMEM((classes, b7, 2 * b7), BF16),
        pltpu.VMEM((classes, block, depth), BF16),
        pltpu.VMEM((b7, r), F32),
        pltpu.VMEM((r // 128, 64, 128), F32),
        pltpu.VMEM((r // 128, b7, 128), F32),
        pltpu.SemaphoreType.DMA((10,)),
        pltpu.SemaphoreType.DMA((4,)),
        pltpu.SemaphoreType.DMA((4,)),
        pltpu.SemaphoreType.DMA,
        pltpu.SemaphoreType.DMA,
    ]
    return pl.pallas_call(
        functools.partial(kernel, (axes, counts, classes, nb4, nb3)),
        out_shape=pltpu.VMEM((expd.shape[0], b7), F32),
        in_specs=[pl.BlockSpec(memory_space=pltpu.HBM)] * len(args),
        out_specs=pl.BlockSpec(memory_space=pltpu.VMEM),
        scratch_shapes=scratch,
        compiler_params=pltpu.CompilerParams(
            collective_id=0, has_side_effects=True, vmem_limit_bytes=50 * 1024 * 1024
        ),
    )(*[pltpu.with_memory_space_constraint(a, pltpu.HBM) for a in args])


def solution(mesh):
    axes = tuple(mesh.axis_names)
    counts = tuple(mesh.shape[a] for a in axes)
    cut = P(None, axes)
    return jax.shard_map(
        functools.partial(on_device, axes, counts),
        mesh=mesh,
        in_specs=(cut, P(), P(), P(), P(), cut, cut, cut, P(), P()),
        out_specs=cut,
        check_vma=False,
    )
```

```python
import functools
import itertools

import jax
import jax.numpy as jnp
from jax import lax
from jax.experimental import pallas as pl
from jax.experimental.pallas import tpu as pltpu
from jax.sharding import PartitionSpec as P

MESH = pl.DeviceIdType.MESH
F32 = jnp.float32
BF16 = jnp.bfloat16


def nt(a, b):
    return lax.dot_general(a, b, (((1,), (1,)), ((), ())), preferred_element_type=F32)


def tn(a, b):
    return lax.dot_general(a, b, (((0,), (0,)), ((), ())), preferred_element_type=F32)


def nn(a, b):
    return jnp.dot(a, b, preferred_element_type=F32)


def iota(shape, axis):
    return lax.broadcasted_iota(jnp.int32, shape, axis)


def take_rows(ref, start, rows, stride=1):
    parts = [ref[h, pl.ds(start, rows, stride=stride), :] for h in range(ref.shape[0])]
    return jnp.concatenate(parts, axis=1)


def put_rows(ref, start, rows, value, stride=1):
    for h in range(ref.shape[0]):
        ref[h, pl.ds(start, rows, stride=stride), :] = value[:, h * 128 : (h + 1) * 128]


def onehot(column, width, start=0):
    rows = column.shape[0]
    return jnp.where(iota((rows, width), 1) + start == column, 1.0, 0.0).astype(BF16)


def column(row, rows):
    shape = (rows, row.shape[1])
    spread_row = jnp.where(iota(shape, 0) == iota(shape, 1), row, -1.0)
    return jnp.max(spread_row, axis=1, keepdims=True)


def kernel(
    sizes,
    mult_h,
    comp_h,
    octs_h,
    fars_h,
    l7_h,
    l6_h,
    l5_h,
    l4_h,
    l3_h,
    local_ref,
    mult,
    comp,
    octs,
    fars,
    l7,
    l6,
    l5,
    l4,
    l3,
    c7f,
    c6f,
    c4f,
    own,
    halo,
    small,
    every,
    own_pick,
    hot,
    hot_small,
    acc,
    d6,
    d7,
    load_sem,
    send_sem,
    recv_sem,
    all_send,
    all_recv,
):
    axes, counts, classes, nb4, nb3 = sizes
    n = counts[0] * counts[1]
    b7 = c7f.shape[1]
    b6 = b7 // 8
    b5 = b6 // 8
    per4 = 8 // b5
    block = b6 + 16
    me = lax.axis_index(axes[0]) * counts[1] + lax.axis_index(axes[1])

    def place(peer):
        return (peer // counts[1], peer % counts[1])

    loads = [
        pltpu.make_async_copy(src, dst, load_sem.at[k])
        for k, (src, dst) in enumerate(
            [
                (comp_h, comp),
                (mult_h, mult),
                (octs_h, octs),
                (l7_h, l7),
                (l6_h, l6),
                (l5_h, l5),
                (l4_h, l4),
                (l3_h, l3),
                (fars_h, fars),
            ]
        )
    ]
    for load in loads[:8]:
        load.start()

    barrier = pltpu.get_barrier_semaphore()

    def greet(k, carry):
        pl.semaphore_signal(
            barrier, inc=1, device_id=place(lax.rem(me + k, n)), device_id_type=MESH
        )
        return carry

    lax.fori_loop(1, n, greet, 0)
    c6f[...] = jnp.zeros_like(c6f)
    c4f[...] = jnp.zeros_like(c4f)
    rows3 = c4f.shape[1] // 8
    base4 = 3 * block
    base3 = base4 + nb4
    depth = small.shape[0]
    t4 = me // per4
    t3 = t4 // 8

    loads[0].wait()
    loads[1].wait()
    loads[8].start()
    seven = tn(mult[...], comp[...]).astype(BF16)
    own[...] = seven
    put_rows(c7f, 0, b7, seven.astype(F32))

    pl.semaphore_wait(barrier, n - 1)
    right = place(lax.rem(me + 1, n))
    left = place(lax.rem(me + n - 1, n))

    def halo_copy(src, ref, rows, slot, peer, index):
        return pltpu.make_async_remote_copy(
            src_ref=src,
            dst_ref=ref.at[pl.ds(slot * rows, rows), :],
            send_sem=send_sem.at[index],
            recv_sem=recv_sem.at[index],
            device_id=peer,
            device_id_type=MESH,
        )

    halo_sends = [
        halo_copy(own, halo, b7, 0, right, 0),
        halo_copy(own, halo, b7, 1, left, 1),
    ]
    for copy in halo_sends:
        copy.start()

    loads[2].wait()
    total = jnp.zeros((b6, octs.shape[1]), F32)
    for o in range(8):
        total = total + nt(take_rows(c7f, o, b6, 8).astype(BF16), octs[o])
    six = total.astype(BF16)
    put_rows(c6f, 0, b6, six.astype(F32))
    total = jnp.zeros((16, octs.shape[1]), F32)
    for o in range(8):
        total = total + nt(take_rows(c6f, o, 16, 8).astype(BF16), octs[o])
    five = total.astype(BF16)
    small[block : block + b6, :] = six
    small[block + b6 : 2 * block, :] = five
    fivef = five.astype(F32)
    half = octs.shape[1] // 2
    tile = jnp.concatenate([fivef[0:b5, :half], fivef[0:b5, half:]], axis=0)
    mine = pl.ds(pl.multiple_of(me * 8, 8), 8)
    every[mine, :] = tile

    small_sends = [
        halo_copy(small.at[pl.ds(block, block), :], small, block, 0, right, 2),
        halo_copy(small.at[pl.ds(block, block), :], small, block, 2, left, 3),
    ]

    def spread(k):
        pltpu.make_async_remote_copy(
            src_ref=every.at[mine, :],
            dst_ref=every.at[mine, :],
            send_sem=all_send,
            recv_sem=all_recv,
            device_id=place(lax.rem(me + k, n)),
            device_id_type=MESH,
        ).start()

    for copy in small_sends:
        copy.start()
    peers = iter(range(1, n))
    each = -(-2 * (n - 1) // classes)

    for k in range(3, 8):
        loads[k].wait()
    e7 = l7[...]
    p7 = jnp.where(e7 >= 0, e7 - (me * b7 - b7), -1).astype(F32).T.astype(jnp.int32)
    e6 = l6[...]
    p6 = e6 - (me * b6 - b6)
    p6 = p6 + jnp.where(p6 >= b6, block - b6, 0) + jnp.where(p6 >= 2 * b6, block - b6, 0)
    p6 = jnp.where(e6 >= 0, p6, -1).astype(F32)
    e5 = l5[...]
    p5 = e5 - (me * b5 - b5)
    p5 = p5 + b6 + jnp.where(p5 >= b5, block - b5, 0) + jnp.where(p5 >= 2 * b5, block - b5, 0)
    p5 = jnp.where(e5 >= 0, p5, -1)
    p5 = jnp.concatenate([p5, jnp.full((16 - b5, classes), -1, jnp.int32)], axis=0)

    e4 = l4[...]
    p4 = jnp.where(iota(e4.shape, 1) == t4, e4, -1).astype(F32)
    p4 = jnp.max(p4, axis=1, keepdims=True).astype(jnp.int32)
    p4 = jnp.where(p4 >= 0, p4 + base4, -1)
    e3 = l3[...]
    p3 = jnp.where(iota(e3.shape, 0) == t3, e3, -1).astype(F32)
    p3 = column(jnp.max(p3, axis=0, keepdims=True), classes).astype(jnp.int32)
    p3 = jnp.where(p3 >= 0, p3 + base3, -1)
    row = iota((16, 1), 0)

    def pick_own(c):
        own_pick[c] = nn(onehot(p7[:, c : c + 1], b7, b7), own[...]).astype(BF16)

    for c in range(classes):
        for k in itertools.islice(peers, each):
            spread(k)
        col = p7[:, c : c + 1]
        if c < classes // 2:
            pick_own(c)
        hot[c, :, 0:b7] = onehot(col, b7, 0)
        hot[c, :, b7 : 2 * b7] = onehot(col, b7, 2 * b7)
        tail = jnp.where(row == b5, p4[c : c + 1, :], p5[:, c : c + 1])
        tail = jnp.where(row == b5 + 1, p3[c : c + 1, :], tail)
        cols = jnp.concatenate([column(p6[c : c + 1, :], b6).astype(jnp.int32), tail], axis=0)
        hot_small[c] = onehot(cols, depth)

    loads[8].wait()
    rest = every.at[pl.ds(0, (n - 1) * 8), :]
    pltpu.make_async_copy(rest, rest, all_recv).wait()
    for copy in small_sends:
        copy.wait_recv()

    def coarser():
        total = jnp.zeros((nb4, octs.shape[1]), F32)
        for o in range(8):
            at = (o // b5) * 8 + o % b5
            low = every[pl.ds(at, nb4, stride=8 * per4), :]
            high = every[pl.ds(at + b5, nb4, stride=8 * per4), :]
            total = total + nt(jnp.concatenate([low, high], axis=1).astype(BF16), octs[o])
            if o % 4 == 3:
                yield
        four = total.astype(BF16)
        put_rows(c4f, 0, nb4, four.astype(F32))
        small[base4 : base4 + nb4, :] = four
        total = jnp.zeros((rows3, octs.shape[1]), F32)
        for o in range(8):
            total = total + nt(take_rows(c4f, o, rows3, 8).astype(BF16), octs[o])
            if o % 4 == 3:
                yield
        small[base3 : base3 + rows3, :] = total.astype(BF16)
        far = jnp.zeros((block, octs.shape[1]), F32)
        for c in range(classes):
            lesser = nn(hot_small[c], small[...]).astype(BF16)
            far = far + nt(lesser, fars[c])
            if c % 4 == 3:
                yield
        far6, far5 = 2.0 * far[0:b6, :], 4.0 * far[b6:block, :]
        far4 = 8.0 * far[b6 + b5 : b6 + b5 + 1, :]
        far3 = 16.0 * far[b6 + b5 + 1 : b6 + b5 + 2, :]
        wide = (16, octs.shape[1])
        down = nn(jnp.broadcast_to(far3, wide).astype(BF16), octs[t4 % 8])
        local4 = jnp.broadcast_to(far4 + down[0:1, :], wide)
        yield
        local5 = far5
        first = (me % per4) * b5
        for k in range(b5):
            local5 = local5 + nn(
                jnp.where(iota(wide, 0) == k, local4, 0.0).astype(BF16), octs[first + k]
            )
        local5 = local5.astype(BF16)
        yield
        for o in range(8):
            put_rows(d6, o, 8, nn(local5, octs[o])[0:8, :], 8)
        local6 = (far6 + take_rows(d6, 0, b6)).astype(BF16)
        yield
        for o in range(8):
            put_rows(d7, o, b6, nn(local6, octs[o]), 8)
            if o % 4 == 3:
                yield

    chain = coarser()
    for c in range(classes // 2, classes):
        next(chain, None)
        pick_own(c)
    for copy in halo_sends:
        copy.wait_recv()
    for c in range(classes):
        next(chain, None)
        picked = nn(hot[c], halo[...]) + own_pick[c].astype(F32)
        if c == 0:
            acc[...] = nt(picked.astype(BF16), fars[c])
        else:
            acc[...] += nt(picked.astype(BF16), fars[c])
    for _ in chain:
        pass
    local_ref[...] = (acc[...] + take_rows(d7, 0, b7)).astype(BF16)

    for copy in halo_sends + small_sends:
        copy.wait_send()
    pltpu.make_async_copy(rest, rest, all_send).wait()


def on_device(axes, counts, *args):
    mult, comp, expd, octs, fars, l7, l6, l5, l4, l3 = args
    args = (mult, comp.T, octs, fars, l7, l6, l5.T, l4, l3.T)
    n = counts[0] * counts[1]
    b7, b6, b5 = l7.shape[1], l6.shape[1], l5.shape[1]
    nb4, nb3 = l4.shape[1], l3.shape[1]
    classes, r = fars.shape[0], fars.shape[1]
    if b6 * 8 != b7 or b5 * 8 != b6 or b5 != 4 or nb4 % 16:
        raise ValueError("unsupported sizes")
    block = b6 + 16
    rows3 = max(16, nb3)
    depth = 3 * block + nb4 + rows3
    scratch = [pltpu.VMEM(a.shape, a.dtype) for a in args]
    scratch += [
        pltpu.VMEM((r // 128, b7, 128), F32),
        pltpu.VMEM((r // 128, 128, 128), F32),
        pltpu.VMEM((r // 128, rows3 * 8, 128), F32),
        pltpu.VMEM((b7, r), BF16),
        pltpu.VMEM((2 * b7, r), BF16),
        pltpu.VMEM((depth, r), BF16),
        pltpu.VMEM((n * 8, r // 2), F32),
        pltpu.VMEM((classes, b7, r), BF16),
        pltpu.VMEM((classes, b7, 2 * b7), BF16),
        pltpu.VMEM((classes, block, depth), BF16),
        pltpu.VMEM((b7, r), F32),
        pltpu.VMEM((r // 128, 64, 128), F32),
        pltpu.VMEM((r // 128, b7, 128), F32),
        pltpu.SemaphoreType.DMA((9,)),
        pltpu.SemaphoreType.DMA((4,)),
        pltpu.SemaphoreType.DMA((4,)),
        pltpu.SemaphoreType.DMA,
        pltpu.SemaphoreType.DMA,
    ]
    local = pl.pallas_call(
        functools.partial(kernel, (axes, counts, classes, nb4, nb3)),
        out_shape=pltpu.VMEM((b7, r), BF16),
        in_specs=[pl.BlockSpec(memory_space=pltpu.HBM)] * len(args),
        out_specs=pl.BlockSpec(memory_space=pltpu.VMEM),
        scratch_shapes=scratch,
        compiler_params=pltpu.CompilerParams(
            collective_id=0, has_side_effects=True, vmem_limit_bytes=50 * 1024 * 1024
        ),
    )(*[pltpu.with_memory_space_constraint(a, pltpu.HBM) for a in args])
    return nt(expd, local)


def solution(mesh):
    axes = tuple(mesh.axis_names)
    counts = tuple(mesh.shape[a] for a in axes)
    cut = P(None, axes)
    return jax.shard_map(
        functools.partial(on_device, axes, counts),
        mesh=mesh,
        in_specs=(cut, P(), P(), P(), P(), cut, cut, cut, P(), P()),
        out_specs=cut,
        check_vma=False,
    )
```

```python
import functools
import itertools

import jax
import jax.numpy as jnp
from jax import lax
from jax.experimental import pallas as pl
from jax.experimental.pallas import tpu as pltpu
from jax.sharding import PartitionSpec as P

MESH = pl.DeviceIdType.MESH
F32 = jnp.float32
BF16 = jnp.bfloat16


def nt(a, b):
    return lax.dot_general(a, b, (((1,), (1,)), ((), ())), preferred_element_type=F32)


def tn(a, b):
    return lax.dot_general(a, b, (((0,), (0,)), ((), ())), preferred_element_type=F32)


def nn(a, b):
    return jnp.dot(a, b, preferred_element_type=F32)


def iota(shape, axis):
    return lax.broadcasted_iota(jnp.int32, shape, axis)


def beside(parts):
    return jnp.concatenate(list(parts), axis=1)


def lanes_of(ops):
    return beside(ops[k] for k in range(ops.shape[0]))


def take_rows(ref, start, rows, stride=1):
    parts = [ref[h, pl.ds(start, rows, stride=stride), :] for h in range(ref.shape[0])]
    return jnp.concatenate(parts, axis=1)


def put_rows(ref, start, rows, value, stride=1):
    for h in range(ref.shape[0]):
        ref[h, pl.ds(start, rows, stride=stride), :] = value[:, h * 128 : (h + 1) * 128]


def onehot(column, width, start=0):
    rows = column.shape[0]
    return jnp.where(iota((rows, width), 1) + start == column, 1.0, 0.0).astype(BF16)


def column(row, rows):
    shape = (rows, row.shape[1])
    spread_row = jnp.where(iota(shape, 0) == iota(shape, 1), row, -1.0)
    return jnp.max(spread_row, axis=1, keepdims=True)


def kernel(
    sizes,
    mult_h,
    comp_h,
    octs_h,
    fars_h,
    l7_h,
    l6_h,
    l5_h,
    l4_h,
    l3_h,
    local_ref,
    mult,
    comp,
    octs,
    fars,
    l7,
    l6,
    l5,
    l4,
    l3,
    c7f,
    c6f,
    c4f,
    own,
    halo,
    small,
    every,
    own_pick,
    hot_own,
    hot,
    hot_small,
    acc,
    d6,
    d7,
    load_sem,
    send_sem,
    recv_sem,
    all_send,
    all_recv,
):
    axes, counts, classes, nb4, nb3 = sizes
    n = counts[0] * counts[1]
    b7 = c7f.shape[1]
    b6 = b7 // 8
    b5 = b6 // 8
    per4 = 8 // b5
    block = b6 + 16
    me = lax.axis_index(axes[0]) * counts[1] + lax.axis_index(axes[1])

    def place(peer):
        return (peer // counts[1], peer % counts[1])

    loads = [
        pltpu.make_async_copy(src, dst, load_sem.at[k])
        for k, (src, dst) in enumerate(
            [
                (comp_h, comp),
                (mult_h, mult),
                (octs_h, octs),
                (l7_h, l7),
                (l6_h, l6),
                (l5_h, l5),
                (l4_h, l4),
                (l3_h, l3),
                (fars_h, fars),
            ]
        )
    ]
    for load in loads[:8]:
        load.start()

    barrier = pltpu.get_barrier_semaphore()

    def greet(k, carry):
        pl.semaphore_signal(
            barrier, inc=1, device_id=place(lax.rem(me + k, n)), device_id_type=MESH
        )
        return carry

    lax.fori_loop(1, n, greet, 0)
    c6f[...] = jnp.zeros_like(c6f)
    c4f[...] = jnp.zeros_like(c4f)
    rows3 = c4f.shape[1] // 8
    base4 = 3 * block
    base3 = base4 + nb4
    depth = small.shape[0]
    t4 = me // per4
    t3 = t4 // 8

    loads[0].wait()
    loads[1].wait()
    loads[8].start()
    seven = tn(mult[...], comp[...]).astype(BF16)
    own[...] = seven
    put_rows(c7f, 0, b7, seven.astype(F32))

    pl.semaphore_wait(barrier, n - 1)
    right = place(lax.rem(me + 1, n))
    left = place(lax.rem(me + n - 1, n))

    def halo_copy(src, ref, rows, slot, peer, index):
        return pltpu.make_async_remote_copy(
            src_ref=src,
            dst_ref=ref.at[pl.ds(slot * rows, rows), :],
            send_sem=send_sem.at[index],
            recv_sem=recv_sem.at[index],
            device_id=peer,
            device_id_type=MESH,
        )

    halo_sends = [
        halo_copy(own, halo, b7, 0, right, 0),
        halo_copy(own, halo, b7, 1, left, 1),
    ]
    for copy in halo_sends:
        copy.start()

    loads[2].wait()
    up = lanes_of(octs)
    six = nt(beside(take_rows(c7f, o, b6, 8).astype(BF16) for o in range(8)), up).astype(BF16)
    put_rows(c6f, 0, b6, six.astype(F32))
    five = nt(beside(take_rows(c6f, o, 16, 8).astype(BF16) for o in range(8)), up).astype(BF16)
    small[block : block + b6, :] = six
    small[block + b6 : 2 * block, :] = five
    fivef = five.astype(F32)
    half = octs.shape[1] // 2
    tile = jnp.concatenate([fivef[0:b5, :half], fivef[0:b5, half:]], axis=0)
    mine = pl.ds(pl.multiple_of(me * 8, 8), 8)
    every[mine, :] = tile

    small_sends = [
        halo_copy(small.at[pl.ds(block, block), :], small, block, 0, right, 2),
        halo_copy(small.at[pl.ds(block, block), :], small, block, 2, left, 3),
    ]

    def spread(k):
        pltpu.make_async_remote_copy(
            src_ref=every.at[mine, :],
            dst_ref=every.at[mine, :],
            send_sem=all_send,
            recv_sem=all_recv,
            device_id=place(lax.rem(me + k, n)),
            device_id_type=MESH,
        ).start()

    for copy in small_sends:
        copy.start()
    peers = iter(range(1, n))
    each = -(-4 * (n - 1) // classes)

    for k in range(3, 8):
        loads[k].wait()
    e7 = l7[...]
    p7 = jnp.where(e7 >= 0, e7 - (me * b7 - b7), -1).astype(F32).T.astype(jnp.int32)
    e6 = l6[...]
    p6 = e6 - (me * b6 - b6)
    p6 = p6 + jnp.where(p6 >= b6, block - b6, 0) + jnp.where(p6 >= 2 * b6, block - b6, 0)
    p6 = jnp.where(e6 >= 0, p6, -1).astype(F32)
    e5 = l5[...]
    p5 = e5 - (me * b5 - b5)
    p5 = p5 + b6 + jnp.where(p5 >= b5, block - b5, 0) + jnp.where(p5 >= 2 * b5, block - b5, 0)
    p5 = jnp.where(e5 >= 0, p5, -1)
    p5 = jnp.concatenate([p5, jnp.full((16 - b5, classes), -1, jnp.int32)], axis=0)

    e4 = l4[...]
    p4 = jnp.where(iota(e4.shape, 1) == t4, e4, -1).astype(F32)
    p4 = jnp.max(p4, axis=1, keepdims=True).astype(jnp.int32)
    p4 = jnp.where(p4 >= 0, p4 + base4, -1)
    e3 = l3[...]
    p3 = jnp.where(iota(e3.shape, 0) == t3, e3, -1).astype(F32)
    p3 = column(jnp.max(p3, axis=0, keepdims=True), classes).astype(jnp.int32)
    p3 = jnp.where(p3 >= 0, p3 + base3, -1)
    row = iota((16, 1), 0)

    group = 4

    for c in range(classes):
        for k in itertools.islice(peers, each):
            spread(k)
        col = p7[:, c : c + 1]
        rows = pl.ds(c * b7, b7)
        hot_own[rows, :] = onehot(col, b7, b7)
        hot[rows, 0:b7] = onehot(col, b7, 0)
        hot[rows, b7 : 2 * b7] = onehot(col, b7, 2 * b7)
        tail = jnp.where(row == b5, p4[c : c + 1, :], p5[:, c : c + 1])
        tail = jnp.where(row == b5 + 1, p3[c : c + 1, :], tail)
        cols = jnp.concatenate([column(p6[c : c + 1, :], b6).astype(jnp.int32), tail], axis=0)
        hot_small[c * block : (c + 1) * block, :] = onehot(cols, depth)
        if c % group == group - 1:
            rows = pl.ds((c + 1 - group) * b7, group * b7)
            own_pick[rows, :] = nn(hot_own[rows, :], own[...]).astype(BF16)

    loads[8].wait()
    rest = every.at[pl.ds(0, (n - 1) * 8), :]
    pltpu.make_async_copy(rest, rest, all_recv).wait()
    for copy in halo_sends + small_sends:
        copy.wait_recv()

    def coarser():
        parts = []
        for o in range(8):
            at = (o // b5) * 8 + o % b5
            low = every[pl.ds(at, nb4, stride=8 * per4), :]
            high = every[pl.ds(at + b5, nb4, stride=8 * per4), :]
            parts += [low.astype(BF16), high.astype(BF16)]
        four = nt(beside(parts), up).astype(BF16)
        put_rows(c4f, 0, nb4, four.astype(F32))
        small[base4 : base4 + nb4, :] = four
        yield
        parts = [take_rows(c4f, o, rows3, 8).astype(BF16) for o in range(8)]
        small[base3 : base3 + rows3, :] = nt(beside(parts), up).astype(BF16)
        yield
        lesser = nn(hot_small[...], small[...]).astype(BF16)
        lesser = beside(lesser[c * block : (c + 1) * block, :] for c in range(classes))
        far = nt(lesser, lanes_of(fars))
        yield
        far6, far5 = 2.0 * far[0:b6, :], 4.0 * far[b6:block, :]
        far4 = 8.0 * far[b6 + b5 : b6 + b5 + 1, :]
        far3 = 16.0 * far[b6 + b5 + 1 : b6 + b5 + 2, :]
        wide = (16, octs.shape[1])
        down = nn(jnp.broadcast_to(far3, wide).astype(BF16), octs[t4 % 8])
        local4 = jnp.broadcast_to(far4 + down[0:1, :], wide)
        yield
        first = (me % per4) * b5
        parts = [jnp.where(iota(wide, 0) == k, local4, 0.0).astype(BF16) for k in range(b5)]
        ops = octs[pl.ds(first, b5)].reshape(b5 * wide[1], wide[1])
        local5 = far5 + nn(beside(parts), ops)
        local5 = local5.astype(BF16)
        yield
        for o in range(8):
            put_rows(d6, o, 8, nn(local5, octs[o])[0:8, :], 8)
        local6 = (far6 + take_rows(d6, 0, b6)).astype(BF16)
        yield
        for o in range(8):
            put_rows(d7, o, b6, nn(local6, octs[o]), 8)
            if o % 4 == 3:
                yield

    chain = coarser()
    for start in range(0, classes, group):
        next(chain, None)
        rows = pl.ds(start * b7, group * b7)
        picked = (nn(hot[rows, :], halo[...]) + own_pick[rows, :].astype(F32)).astype(BF16)
        next(chain, None)
        wide_picked = beside(picked[k * b7 : (k + 1) * b7, :] for k in range(group))
        far = nt(wide_picked, lanes_of(fars.at[pl.ds(start, group)]))
        acc[...] = far if start == 0 else acc[...] + far
    for _ in chain:
        pass
    local_ref[...] = (acc[...] + take_rows(d7, 0, b7)).astype(BF16)

    for copy in halo_sends + small_sends:
        copy.wait_send()
    pltpu.make_async_copy(rest, rest, all_send).wait()


def on_device(axes, counts, *args):
    mult, comp, expd, octs, fars, l7, l6, l5, l4, l3 = args
    args = (mult, comp.T, octs, fars, l7, l6, l5.T, l4, l3.T)
    n = counts[0] * counts[1]
    b7, b6, b5 = l7.shape[1], l6.shape[1], l5.shape[1]
    nb4, nb3 = l4.shape[1], l3.shape[1]
    classes, r = fars.shape[0], fars.shape[1]
    if b6 * 8 != b7 or b5 * 8 != b6 or b5 != 4 or nb4 % 16:
        raise ValueError("unsupported sizes")
    block = b6 + 16
    rows3 = max(16, nb3)
    depth = 3 * block + nb4 + rows3
    scratch = [pltpu.VMEM(a.shape, a.dtype) for a in args]
    scratch += [
        pltpu.VMEM((r // 128, b7, 128), F32),
        pltpu.VMEM((r // 128, 128, 128), F32),
        pltpu.VMEM((r // 128, rows3 * 8, 128), F32),
        pltpu.VMEM((b7, r), BF16),
        pltpu.VMEM((2 * b7, r), BF16),
        pltpu.VMEM((depth, r), BF16),
        pltpu.VMEM((n * 8, r // 2), F32),
        pltpu.VMEM((classes * b7, r), BF16),
        pltpu.VMEM((classes * b7, b7), BF16),
        pltpu.VMEM((classes * b7, 2 * b7), BF16),
        pltpu.VMEM((classes * block, depth), BF16),
        pltpu.VMEM((b7, r), F32),
        pltpu.VMEM((r // 128, 64, 128), F32),
        pltpu.VMEM((r // 128, b7, 128), F32),
        pltpu.SemaphoreType.DMA((9,)),
        pltpu.SemaphoreType.DMA((4,)),
        pltpu.SemaphoreType.DMA((4,)),
        pltpu.SemaphoreType.DMA,
        pltpu.SemaphoreType.DMA,
    ]
    local = pl.pallas_call(
        functools.partial(kernel, (axes, counts, classes, nb4, nb3)),
        out_shape=pltpu.VMEM((b7, r), BF16),
        in_specs=[pl.BlockSpec(memory_space=pltpu.HBM)] * len(args),
        out_specs=pl.BlockSpec(memory_space=pltpu.VMEM),
        scratch_shapes=scratch,
        compiler_params=pltpu.CompilerParams(
            collective_id=0, has_side_effects=True, vmem_limit_bytes=50 * 1024 * 1024
        ),
    )(*[pltpu.with_memory_space_constraint(a, pltpu.HBM) for a in args])
    return nt(expd, local)


def solution(mesh):
    axes = tuple(mesh.axis_names)
    counts = tuple(mesh.shape[a] for a in axes)
    cut = P(None, axes)
    return jax.shard_map(
        functools.partial(on_device, axes, counts),
        mesh=mesh,
        in_specs=(cut, P(), P(), P(), P(), cut, cut, cut, P(), P()),
        out_specs=cut,
        check_vma=False,
    )
```

```python
import functools
import itertools

import jax
import jax.numpy as jnp
from jax import lax
from jax.experimental import pallas as pl
from jax.experimental.pallas import tpu as pltpu
from jax.sharding import PartitionSpec as P

MESH = pl.DeviceIdType.MESH
F32 = jnp.float32
BF16 = jnp.bfloat16


def nt(a, b):
    return lax.dot_general(a, b, (((1,), (1,)), ((), ())), preferred_element_type=F32)


def tn(a, b):
    return lax.dot_general(a, b, (((0,), (0,)), ((), ())), preferred_element_type=F32)


def nn(a, b):
    return jnp.dot(a, b, preferred_element_type=F32)


def iota(shape, axis):
    return lax.broadcasted_iota(jnp.int32, shape, axis)


def beside(parts):
    return jnp.concatenate(list(parts), axis=1)


def lanes_of(ops):
    return beside(ops[k] for k in range(ops.shape[0]))


def take_rows(ref, start, rows, stride=1):
    parts = [ref[h, pl.ds(start, rows, stride=stride), :] for h in range(ref.shape[0])]
    return jnp.concatenate(parts, axis=1)


def put_rows(ref, start, rows, value, stride=1):
    for h in range(ref.shape[0]):
        ref[h, pl.ds(start, rows, stride=stride), :] = value[:, h * 128 : (h + 1) * 128]


def onehot(column, width, start=0):
    rows = column.shape[0]
    return jnp.where(iota((rows, width), 1) + start == column, 1.0, 0.0).astype(BF16)


def column(row, rows):
    shape = (rows, row.shape[1])
    spread_row = jnp.where(iota(shape, 0) == iota(shape, 1), row, -1.0)
    return jnp.max(spread_row, axis=1, keepdims=True)


def kernel(
    sizes,
    mult_h,
    comp_h,
    octs_h,
    fars_h,
    l7_h,
    l6_h,
    l5_h,
    l4_h,
    l3_h,
    local_ref,
    mult,
    comp,
    octs,
    fars,
    l7,
    l6,
    l5,
    l4,
    l3,
    c7f,
    c6f,
    c4f,
    own,
    halo,
    small,
    every,
    own_pick,
    hot_own,
    hot,
    hot_small,
    acc,
    d6,
    d7,
    load_sem,
    send_sem,
    recv_sem,
    all_send,
    all_recv,
):
    axes, counts, classes, nb4, nb3 = sizes
    n = counts[0] * counts[1]
    b7 = c7f.shape[1]
    b6 = b7 // 8
    b5 = b6 // 8
    per4 = 8 // b5
    block = b6 + 16
    me = lax.axis_index(axes[0]) * counts[1] + lax.axis_index(axes[1])

    def place(peer):
        return (peer // counts[1], peer % counts[1])

    loads = [
        pltpu.make_async_copy(src, dst, load_sem.at[k])
        for k, (src, dst) in enumerate(
            [
                (comp_h, comp),
                (mult_h, mult),
                (octs_h, octs),
                (l7_h, l7),
                (l6_h, l6),
                (l5_h, l5),
                (l4_h, l4),
                (l3_h, l3),
                (fars_h, fars),
            ]
        )
    ]
    for load in loads[:8]:
        load.start()

    barrier = pltpu.get_barrier_semaphore()

    def greet(k, carry):
        pl.semaphore_signal(
            barrier, inc=1, device_id=place(lax.rem(me + k, n)), device_id_type=MESH
        )
        return carry

    lax.fori_loop(1, n, greet, 0)
    c6f[...] = jnp.zeros_like(c6f)
    c4f[...] = jnp.zeros_like(c4f)
    rows3 = c4f.shape[1] // 8
    base4 = 3 * block
    base3 = base4 + nb4
    depth = small.shape[0]
    t4 = me // per4
    t3 = t4 // 8

    loads[0].wait()
    loads[1].wait()
    loads[8].start()
    seven = tn(mult[...], comp[...]).astype(BF16)
    own[...] = seven
    put_rows(c7f, 0, b7, seven.astype(F32))

    pl.semaphore_wait(barrier, n - 1)
    right = place(lax.rem(me + 1, n))
    left = place(lax.rem(me + n - 1, n))

    def halo_copy(src, ref, rows, slot, peer, index):
        return pltpu.make_async_remote_copy(
            src_ref=src,
            dst_ref=ref.at[pl.ds(slot * rows, rows), :],
            send_sem=send_sem.at[index],
            recv_sem=recv_sem.at[index],
            device_id=peer,
            device_id_type=MESH,
        )

    halo_sends = [
        halo_copy(own, halo, b7, 0, right, 0),
        halo_copy(own, halo, b7, 1, left, 1),
    ]
    for copy in halo_sends:
        copy.start()

    loads[2].wait()
    up = lanes_of(octs)
    six = nt(beside(take_rows(c7f, o, b6, 8).astype(BF16) for o in range(8)), up).astype(BF16)
    put_rows(c6f, 0, b6, six.astype(F32))
    five = nt(beside(take_rows(c6f, o, 16, 8).astype(BF16) for o in range(8)), up).astype(BF16)
    small[block : block + b6, :] = six
    small[block + b6 : 2 * block, :] = five
    fivef = five.astype(F32)
    half = octs.shape[1] // 2
    tile = jnp.concatenate([fivef[0:b5, :half], fivef[0:b5, half:]], axis=0)
    mine = pl.ds(pl.multiple_of(me * 8, 8), 8)
    every[mine, :] = tile

    small_sends = [
        halo_copy(small.at[pl.ds(block, block), :], small, block, 0, right, 2),
        halo_copy(small.at[pl.ds(block, block), :], small, block, 2, left, 3),
    ]

    def spread(k):
        pltpu.make_async_remote_copy(
            src_ref=every.at[mine, :],
            dst_ref=every.at[mine, :],
            send_sem=all_send,
            recv_sem=all_recv,
            device_id=place(lax.rem(me + k, n)),
            device_id_type=MESH,
        ).start()

    for copy in small_sends:
        copy.start()
    peers = iter(range(1, n))
    each = -(-4 * (n - 1) // classes)

    for k in range(3, 8):
        loads[k].wait()
    e7 = l7[...]
    p7 = jnp.where(e7 >= 0, e7 - (me * b7 - b7), -1).astype(F32).T.astype(jnp.int32)
    e6 = l6[...]
    p6 = e6 - (me * b6 - b6)
    p6 = p6 + jnp.where(p6 >= b6, block - b6, 0) + jnp.where(p6 >= 2 * b6, block - b6, 0)
    p6 = jnp.where(e6 >= 0, p6, -1).astype(F32)
    e5 = l5[...]
    p5 = e5 - (me * b5 - b5)
    p5 = p5 + b6 + jnp.where(p5 >= b5, block - b5, 0) + jnp.where(p5 >= 2 * b5, block - b5, 0)
    p5 = jnp.where(e5 >= 0, p5, -1)
    p5 = jnp.concatenate([p5, jnp.full((16 - b5, classes), -1, jnp.int32)], axis=0)

    e4 = l4[...]
    p4 = jnp.where(iota(e4.shape, 1) == t4, e4, -1).astype(F32)
    p4 = jnp.max(p4, axis=1, keepdims=True).astype(jnp.int32)
    p4 = jnp.where(p4 >= 0, p4 + base4, -1)
    e3 = l3[...]
    p3 = jnp.where(iota(e3.shape, 0) == t3, e3, -1).astype(F32)
    p3 = column(jnp.max(p3, axis=0, keepdims=True), classes).astype(jnp.int32)
    p3 = jnp.where(p3 >= 0, p3 + base3, -1)
    row = iota((16, 1), 0)

    group = 4
    lane7 = iota((b7, b7), 1).astype(jnp.int16)
    one, zero = jnp.ones((b7, b7), BF16), jnp.zeros((b7, b7), BF16)

    for c in range(classes):
        for k in itertools.islice(peers, each):
            spread(k)
        col = jnp.broadcast_to(p7[:, c : c + 1], (b7, b7)).astype(jnp.int16)
        rows = pl.ds(c * b7, b7)
        hot_own[rows, :] = jnp.where(col == lane7 + b7, one, zero)
        hot[rows, 0:b7] = jnp.where(col == lane7, one, zero)
        hot[rows, b7 : 2 * b7] = jnp.where(col == lane7 + 2 * b7, one, zero)
        tail = jnp.where(row == b5, p4[c : c + 1, :], p5[:, c : c + 1])
        tail = jnp.where(row == b5 + 1, p3[c : c + 1, :], tail)
        cols = jnp.concatenate([column(p6[c : c + 1, :], b6).astype(jnp.int32), tail], axis=0)
        hot_small[c * block : (c + 1) * block, :] = onehot(cols, depth)
        if c % group == group - 1:
            rows = pl.ds((c + 1 - group) * b7, group * b7)
            own_pick[rows, :] = nn(hot_own[rows, :], own[...]).astype(BF16)

    loads[8].wait()
    for copy in halo_sends:
        copy.wait_recv()

    def coarser():
        parts = []
        for o in range(8):
            at = (o // b5) * 8 + o % b5
            low = every[pl.ds(at, nb4, stride=8 * per4), :]
            high = every[pl.ds(at + b5, nb4, stride=8 * per4), :]
            parts += [low.astype(BF16), high.astype(BF16)]
        four = nt(beside(parts), up).astype(BF16)
        put_rows(c4f, 0, nb4, four.astype(F32))
        small[base4 : base4 + nb4, :] = four
        yield
        parts = [take_rows(c4f, o, rows3, 8).astype(BF16) for o in range(8)]
        small[base3 : base3 + rows3, :] = nt(beside(parts), up).astype(BF16)
        yield
        lesser = nn(hot_small[...], small[...]).astype(BF16)
        lesser = beside(lesser[c * block : (c + 1) * block, :] for c in range(classes))
        far = nt(lesser, lanes_of(fars))
        yield
        far6, far5 = 2.0 * far[0:b6, :], 4.0 * far[b6:block, :]
        far4 = 8.0 * far[b6 + b5 : b6 + b5 + 1, :]
        far3 = 16.0 * far[b6 + b5 + 1 : b6 + b5 + 2, :]
        wide = (16, octs.shape[1])
        down = nn(jnp.broadcast_to(far3, wide).astype(BF16), octs[t4 % 8])
        local4 = jnp.broadcast_to(far4 + down[0:1, :], wide)
        yield
        first = (me % per4) * b5
        parts = [jnp.where(iota(wide, 0) == k, local4, 0.0).astype(BF16) for k in range(b5)]
        ops = octs[pl.ds(first, b5)].reshape(b5 * wide[1], wide[1])
        local5 = far5 + nn(beside(parts), ops)
        local5 = local5.astype(BF16)
        yield
        for o in range(8):
            put_rows(d6, o, 8, nn(local5, octs[o])[0:8, :], 8)
        local6 = (far6 + take_rows(d6, 0, b6)).astype(BF16)
        yield
        for o in range(8):
            put_rows(d7, o, b6, nn(local6, octs[o]), 8)
            if o % 4 == 3:
                yield

    rest = every.at[pl.ds(0, (n - 1) * 8), :]
    chain = coarser()
    for start in range(0, classes, group):
        if start == group:
            pltpu.make_async_copy(rest, rest, all_recv).wait()
            for copy in small_sends:
                copy.wait_recv()
        if start >= group:
            next(chain, None)
        rows = pl.ds(start * b7, group * b7)
        picked = (nn(hot[rows, :], halo[...]) + own_pick[rows, :].astype(F32)).astype(BF16)
        if start >= group:
            next(chain, None)
        wide_picked = beside(picked[k * b7 : (k + 1) * b7, :] for k in range(group))
        far = nt(wide_picked, lanes_of(fars.at[pl.ds(start, group)]))
        acc[...] = far if start == 0 else acc[...] + far
    for _ in chain:
        pass
    local_ref[...] = (acc[...] + take_rows(d7, 0, b7)).astype(BF16)

    for copy in halo_sends + small_sends:
        copy.wait_send()
    pltpu.make_async_copy(rest, rest, all_send).wait()


def on_device(axes, counts, *args):
    mult, comp, expd, octs, fars, l7, l6, l5, l4, l3 = args
    args = (mult, comp.T, octs, fars, l7, l6, l5.T, l4, l3.T)
    n = counts[0] * counts[1]
    b7, b6, b5 = l7.shape[1], l6.shape[1], l5.shape[1]
    nb4, nb3 = l4.shape[1], l3.shape[1]
    classes, r = fars.shape[0], fars.shape[1]
    if b6 * 8 != b7 or b5 * 8 != b6 or b5 != 4 or nb4 % 16:
        raise ValueError("unsupported sizes")
    block = b6 + 16
    rows3 = max(16, nb3)
    depth = 3 * block + nb4 + rows3
    scratch = [pltpu.VMEM(a.shape, a.dtype) for a in args]
    scratch += [
        pltpu.VMEM((r // 128, b7, 128), F32),
        pltpu.VMEM((r // 128, 128, 128), F32),
        pltpu.VMEM((r // 128, rows3 * 8, 128), F32),
        pltpu.VMEM((b7, r), BF16),
        pltpu.VMEM((2 * b7, r), BF16),
        pltpu.VMEM((depth, r), BF16),
        pltpu.VMEM((n * 8, r // 2), F32),
        pltpu.VMEM((classes * b7, r), BF16),
        pltpu.VMEM((classes * b7, b7), BF16),
        pltpu.VMEM((classes * b7, 2 * b7), BF16),
        pltpu.VMEM((classes * block, depth), BF16),
        pltpu.VMEM((b7, r), F32),
        pltpu.VMEM((r // 128, 64, 128), F32),
        pltpu.VMEM((r // 128, b7, 128), F32),
        pltpu.SemaphoreType.DMA((9,)),
        pltpu.SemaphoreType.DMA((4,)),
        pltpu.SemaphoreType.DMA((4,)),
        pltpu.SemaphoreType.DMA,
        pltpu.SemaphoreType.DMA,
    ]
    local = pl.pallas_call(
        functools.partial(kernel, (axes, counts, classes, nb4, nb3)),
        out_shape=pltpu.VMEM((b7, r), BF16),
        in_specs=[pl.BlockSpec(memory_space=pltpu.HBM)] * len(args),
        out_specs=pl.BlockSpec(memory_space=pltpu.VMEM),
        scratch_shapes=scratch,
        compiler_params=pltpu.CompilerParams(
            collective_id=0, has_side_effects=True, vmem_limit_bytes=50 * 1024 * 1024
        ),
    )(*[pltpu.with_memory_space_constraint(a, pltpu.HBM) for a in args])
    return nt(expd, local)


def solution(mesh):
    axes = tuple(mesh.axis_names)
    counts = tuple(mesh.shape[a] for a in axes)
    cut = P(None, axes)
    return jax.shard_map(
        functools.partial(on_device, axes, counts),
        mesh=mesh,
        in_specs=(cut, P(), P(), P(), P(), cut, cut, cut, P(), P()),
        out_specs=cut,
        check_vma=False,
    )
```

```python
import functools
import itertools

import jax
import jax.numpy as jnp
from jax import lax
from jax.experimental import pallas as pl
from jax.experimental.pallas import tpu as pltpu
from jax.sharding import PartitionSpec as P

MESH = pl.DeviceIdType.MESH
F32 = jnp.float32
BF16 = jnp.bfloat16


def nt(a, b):
    return lax.dot_general(a, b, (((1,), (1,)), ((), ())), preferred_element_type=F32)


def tn(a, b):
    return lax.dot_general(a, b, (((0,), (0,)), ((), ())), preferred_element_type=F32)


def nn(a, b):
    return jnp.dot(a, b, preferred_element_type=F32)


def iota(shape, axis):
    return lax.broadcasted_iota(jnp.int32, shape, axis)


def beside(parts):
    return jnp.concatenate(list(parts), axis=1)


def lanes_of(ops):
    return beside(ops[k] for k in range(ops.shape[0]))


def take_rows(ref, start, rows, stride=1):
    parts = [ref[h, pl.ds(start, rows, stride=stride), :] for h in range(ref.shape[0])]
    return jnp.concatenate(parts, axis=1)


def put_rows(ref, start, rows, value, stride=1):
    for h in range(ref.shape[0]):
        ref[h, pl.ds(start, rows, stride=stride), :] = value[:, h * 128 : (h + 1) * 128]


def onehot(column, width, start=0):
    rows = column.shape[0]
    return jnp.where(iota((rows, width), 1) + start == column, 1.0, 0.0).astype(BF16)


def column(row, rows):
    shape = (rows, row.shape[1])
    spread_row = jnp.where(iota(shape, 0) == iota(shape, 1), row, -1.0)
    return jnp.max(spread_row, axis=1, keepdims=True)


def kernel(
    sizes,
    mult_h,
    comp_h,
    octs_h,
    fars_h,
    l7_h,
    l6_h,
    l5_h,
    l4_h,
    l3_h,
    local_ref,
    mult,
    comp,
    octs,
    fars,
    l7,
    l6,
    l5,
    l4,
    l3,
    c7f,
    c6f,
    c4f,
    own,
    halo,
    small,
    every,
    own_pick,
    hot_own,
    hot,
    hot_small,
    acc,
    d6,
    d7,
    load_sem,
    send_sem,
    recv_sem,
    all_send,
    all_recv,
):
    axes, counts, classes, nb4, nb3 = sizes
    n = counts[0] * counts[1]
    b7 = c7f.shape[1]
    b6 = b7 // 8
    b5 = b6 // 8
    per4 = 8 // b5
    block = b6 + 16
    me = lax.axis_index(axes[0]) * counts[1] + lax.axis_index(axes[1])

    def place(peer):
        return (peer // counts[1], peer % counts[1])

    loads = [
        pltpu.make_async_copy(src, dst, load_sem.at[k])
        for k, (src, dst) in enumerate(
            [
                (comp_h, comp),
                (mult_h, mult),
                (l7_h, l7),
                (l6_h, l6),
                (l5_h, l5),
                (l4_h, l4),
                (l3_h, l3),
                (octs_h, octs),
                (fars_h, fars),
            ]
        )
    ]
    for load in loads[:8]:
        load.start()

    barrier = pltpu.get_barrier_semaphore()

    def greet(k, carry):
        pl.semaphore_signal(
            barrier, inc=1, device_id=place(lax.rem(me + k, n)), device_id_type=MESH
        )
        return carry

    lax.fori_loop(1, n, greet, 0)
    c6f[...] = jnp.zeros_like(c6f)
    c4f[...] = jnp.zeros_like(c4f)
    rows3 = c4f.shape[1] // 8
    base4 = 3 * block
    base3 = base4 + nb4
    depth = small.shape[0]
    t4 = me // per4
    t3 = t4 // 8

    for k in range(2, 7):
        loads[k].wait()
    e7 = l7[...]
    p7 = jnp.where(e7 >= 0, e7 - (me * b7 - b7), -1).astype(F32).T.astype(jnp.int32)
    e6 = l6[...]
    p6 = e6 - (me * b6 - b6)
    p6 = p6 + jnp.where(p6 >= b6, block - b6, 0) + jnp.where(p6 >= 2 * b6, block - b6, 0)
    p6 = jnp.where(e6 >= 0, p6, -1).astype(F32)
    e5 = l5[...]
    p5 = e5 - (me * b5 - b5)
    p5 = p5 + b6 + jnp.where(p5 >= b5, block - b5, 0) + jnp.where(p5 >= 2 * b5, block - b5, 0)
    p5 = jnp.where(e5 >= 0, p5, -1)
    p5 = jnp.concatenate([p5, jnp.full((16 - b5, classes), -1, jnp.int32)], axis=0)

    e4 = l4[...]
    p4 = jnp.where(iota(e4.shape, 1) == t4, e4, -1).astype(F32)
    p4 = jnp.max(p4, axis=1, keepdims=True).astype(jnp.int32)
    p4 = jnp.where(p4 >= 0, p4 + base4, -1)
    e3 = l3[...]
    p3 = jnp.where(iota(e3.shape, 0) == t3, e3, -1).astype(F32)
    p3 = column(jnp.max(p3, axis=0, keepdims=True), classes).astype(jnp.int32)
    p3 = jnp.where(p3 >= 0, p3 + base3, -1)
    row = iota((16, 1), 0)

    group = 4
    lane7 = iota((b7, b7), 1).astype(jnp.int16)
    one, zero = jnp.ones((b7, b7), BF16), jnp.zeros((b7, b7), BF16)

    def build(c):
        col = jnp.broadcast_to(p7[:, c : c + 1], (b7, b7)).astype(jnp.int16)
        rows = pl.ds(c * b7, b7)
        hot_own[rows, :] = jnp.where(col == lane7 + b7, one, zero)
        hot[rows, 0:b7] = jnp.where(col == lane7, one, zero)
        hot[rows, b7 : 2 * b7] = jnp.where(col == lane7 + 2 * b7, one, zero)
        tail = jnp.where(row == b5, p4[c : c + 1, :], p5[:, c : c + 1])
        tail = jnp.where(row == b5 + 1, p3[c : c + 1, :], tail)
        cols = jnp.concatenate([column(p6[c : c + 1, :], b6).astype(jnp.int32), tail], axis=0)
        hot_small[c * block : (c + 1) * block, :] = onehot(cols, depth)

    for c in range(group):
        build(c)

    loads[0].wait()
    loads[1].wait()
    loads[8].start()
    seven = tn(mult[...], comp[...]).astype(BF16)
    own[...] = seven
    put_rows(c7f, 0, b7, seven.astype(F32))

    pl.semaphore_wait(barrier, n - 1)
    right = place(lax.rem(me + 1, n))
    left = place(lax.rem(me + n - 1, n))

    def halo_copy(src, ref, rows, slot, peer, index):
        return pltpu.make_async_remote_copy(
            src_ref=src,
            dst_ref=ref.at[pl.ds(slot * rows, rows), :],
            send_sem=send_sem.at[index],
            recv_sem=recv_sem.at[index],
            device_id=peer,
            device_id_type=MESH,
        )

    halo_sends = [
        halo_copy(own, halo, b7, 0, right, 0),
        halo_copy(own, halo, b7, 1, left, 1),
    ]
    for copy in halo_sends:
        copy.start()

    loads[7].wait()
    up = lanes_of(octs)
    six = nt(beside(take_rows(c7f, o, b6, 8).astype(BF16) for o in range(8)), up).astype(BF16)
    put_rows(c6f, 0, b6, six.astype(F32))
    five = nt(beside(take_rows(c6f, o, 16, 8).astype(BF16) for o in range(8)), up).astype(BF16)
    small[block : block + b6, :] = six
    small[block + b6 : 2 * block, :] = five
    fivef = five.astype(F32)
    half = octs.shape[1] // 2
    tile = jnp.concatenate([fivef[0:b5, :half], fivef[0:b5, half:]], axis=0)
    mine = pl.ds(pl.multiple_of(me * 8, 8), 8)
    every[mine, :] = tile

    small_sends = [
        halo_copy(small.at[pl.ds(block, block), :], small, block, 0, right, 2),
        halo_copy(small.at[pl.ds(block, block), :], small, block, 2, left, 3),
    ]

    def spread(k):
        pltpu.make_async_remote_copy(
            src_ref=every.at[mine, :],
            dst_ref=every.at[mine, :],
            send_sem=all_send,
            recv_sem=all_recv,
            device_id=place(lax.rem(me + k, n)),
            device_id_type=MESH,
        ).start()

    for copy in small_sends:
        copy.start()
    peers = iter(range(1, n))
    each = -(-4 * (n - 1) // classes)

    for c in range(classes):
        for k in itertools.islice(peers, each):
            spread(k)
        if c >= group:
            build(c)
        if c % group == group - 1:
            rows = pl.ds((c + 1 - group) * b7, group * b7)
            own_pick[rows, :] = nn(hot_own[rows, :], own[...]).astype(BF16)

    loads[8].wait()
    for copy in halo_sends:
        copy.wait_recv()

    def coarser():
        parts = []
        for o in range(8):
            at = (o // b5) * 8 + o % b5
            low = every[pl.ds(at, nb4, stride=8 * per4), :]
            high = every[pl.ds(at + b5, nb4, stride=8 * per4), :]
            parts += [low.astype(BF16), high.astype(BF16)]
        four = nt(beside(parts), up).astype(BF16)
        put_rows(c4f, 0, nb4, four.astype(F32))
        small[base4 : base4 + nb4, :] = four
        yield
        parts = [take_rows(c4f, o, rows3, 8).astype(BF16) for o in range(8)]
        small[base3 : base3 + rows3, :] = nt(beside(parts), up).astype(BF16)
        yield
        lesser = nn(hot_small[...], small[...]).astype(BF16)
        lesser = beside(lesser[c * block : (c + 1) * block, :] for c in range(classes))
        far = nt(lesser, lanes_of(fars))
        yield
        far6, far5 = 2.0 * far[0:b6, :], 4.0 * far[b6:block, :]
        far4 = 8.0 * far[b6 + b5 : b6 + b5 + 1, :]
        far3 = 16.0 * far[b6 + b5 + 1 : b6 + b5 + 2, :]
        wide = (16, octs.shape[1])
        down = nn(jnp.broadcast_to(far3, wide).astype(BF16), octs[t4 % 8])
        local4 = jnp.broadcast_to(far4 + down[0:1, :], wide)
        yield
        first = (me % per4) * b5
        parts = [jnp.where(iota(wide, 0) == k, local4, 0.0).astype(BF16) for k in range(b5)]
        ops = octs[pl.ds(first, b5)].reshape(b5 * wide[1], wide[1])
        local5 = far5 + nn(beside(parts), ops)
        local5 = local5.astype(BF16)
        yield
        for o in range(8):
            put_rows(d6, o, 8, nn(local5, octs[o])[0:8, :], 8)
        local6 = (far6 + take_rows(d6, 0, b6)).astype(BF16)
        yield
        for o in range(8):
            put_rows(d7, o, b6, nn(local6, octs[o]), 8)
            if o % 4 == 3:
                yield

    rest = every.at[pl.ds(0, (n - 1) * 8), :]
    chain = coarser()
    for start in range(0, classes, group):
        if start == group:
            pltpu.make_async_copy(rest, rest, all_recv).wait()
            for copy in small_sends:
                copy.wait_recv()
        if start >= group:
            next(chain, None)
        rows = pl.ds(start * b7, group * b7)
        picked = (nn(hot[rows, :], halo[...]) + own_pick[rows, :].astype(F32)).astype(BF16)
        if start >= group:
            next(chain, None)
        wide_picked = beside(picked[k * b7 : (k + 1) * b7, :] for k in range(group))
        far = nt(wide_picked, lanes_of(fars.at[pl.ds(start, group)]))
        acc[...] = far if start == 0 else acc[...] + far
    for _ in chain:
        pass
    local_ref[...] = (acc[...] + take_rows(d7, 0, b7)).astype(BF16)

    for copy in halo_sends + small_sends:
        copy.wait_send()
    pltpu.make_async_copy(rest, rest, all_send).wait()


def on_device(axes, counts, *args):
    mult, comp, expd, octs, fars, l7, l6, l5, l4, l3 = args
    args = (mult, comp.T, octs, fars, l7, l6, l5.T, l4, l3.T)
    n = counts[0] * counts[1]
    b7, b6, b5 = l7.shape[1], l6.shape[1], l5.shape[1]
    nb4, nb3 = l4.shape[1], l3.shape[1]
    classes, r = fars.shape[0], fars.shape[1]
    if b6 * 8 != b7 or b5 * 8 != b6 or b5 != 4 or nb4 % 16:
        raise ValueError("unsupported sizes")
    block = b6 + 16
    rows3 = max(16, nb3)
    depth = 3 * block + nb4 + rows3
    scratch = [pltpu.VMEM(a.shape, a.dtype) for a in args]
    scratch += [
        pltpu.VMEM((r // 128, b7, 128), F32),
        pltpu.VMEM((r // 128, 128, 128), F32),
        pltpu.VMEM((r // 128, rows3 * 8, 128), F32),
        pltpu.VMEM((b7, r), BF16),
        pltpu.VMEM((2 * b7, r), BF16),
        pltpu.VMEM((depth, r), BF16),
        pltpu.VMEM((n * 8, r // 2), F32),
        pltpu.VMEM((classes * b7, r), BF16),
        pltpu.VMEM((classes * b7, b7), BF16),
        pltpu.VMEM((classes * b7, 2 * b7), BF16),
        pltpu.VMEM((classes * block, depth), BF16),
        pltpu.VMEM((b7, r), F32),
        pltpu.VMEM((r // 128, 64, 128), F32),
        pltpu.VMEM((r // 128, b7, 128), F32),
        pltpu.SemaphoreType.DMA((9,)),
        pltpu.SemaphoreType.DMA((4,)),
        pltpu.SemaphoreType.DMA((4,)),
        pltpu.SemaphoreType.DMA,
        pltpu.SemaphoreType.DMA,
    ]
    local = pl.pallas_call(
        functools.partial(kernel, (axes, counts, classes, nb4, nb3)),
        out_shape=pltpu.VMEM((b7, r), BF16),
        in_specs=[pl.BlockSpec(memory_space=pltpu.HBM)] * len(args),
        out_specs=pl.BlockSpec(memory_space=pltpu.VMEM),
        scratch_shapes=scratch,
        compiler_params=pltpu.CompilerParams(
            collective_id=0, has_side_effects=True, vmem_limit_bytes=50 * 1024 * 1024
        ),
    )(*[pltpu.with_memory_space_constraint(a, pltpu.HBM) for a in args])
    return nt(expd, local)


def solution(mesh):
    axes = tuple(mesh.axis_names)
    counts = tuple(mesh.shape[a] for a in axes)
    cut = P(None, axes)
    return jax.shard_map(
        functools.partial(on_device, axes, counts),
        mesh=mesh,
        in_specs=(cut, P(), P(), P(), P(), cut, cut, cut, P(), P()),
        out_specs=cut,
        check_vma=False,
    )
```

```python
import functools
import itertools

import jax
import jax.numpy as jnp
from jax import lax
from jax.experimental import pallas as pl
from jax.experimental.pallas import tpu as pltpu
from jax.sharding import PartitionSpec as P

MESH = pl.DeviceIdType.MESH
F32 = jnp.float32
BF16 = jnp.bfloat16


def nt(a, b):
    return lax.dot_general(a, b, (((1,), (1,)), ((), ())), preferred_element_type=F32)


def tn(a, b):
    return lax.dot_general(a, b, (((0,), (0,)), ((), ())), preferred_element_type=F32)


def nn(a, b):
    return jnp.dot(a, b, preferred_element_type=F32)


def iota(shape, axis):
    return lax.broadcasted_iota(jnp.int32, shape, axis)


def beside(parts):
    return jnp.concatenate(list(parts), axis=1)


def lanes_of(ops):
    return beside(ops[k] for k in range(ops.shape[0]))


def take_rows(ref, start, rows, stride=1):
    parts = [ref[h, pl.ds(start, rows, stride=stride), :] for h in range(ref.shape[0])]
    return jnp.concatenate(parts, axis=1)


def put_rows(ref, start, rows, value, stride=1):
    for h in range(ref.shape[0]):
        ref[h, pl.ds(start, rows, stride=stride), :] = value[:, h * 128 : (h + 1) * 128]


def onehot(column, width, start=0):
    rows = column.shape[0]
    return jnp.where(iota((rows, width), 1) + start == column, 1.0, 0.0).astype(BF16)


def column(row, rows):
    shape = (rows, row.shape[1])
    spread_row = jnp.where(iota(shape, 0) == iota(shape, 1), row, -1.0)
    return jnp.max(spread_row, axis=1, keepdims=True)


def kernel(
    sizes,
    mult_h,
    comp_h,
    octs_h,
    fars_h,
    l7_h,
    l6_h,
    l5_h,
    l4_h,
    l3_h,
    local_ref,
    mult,
    comp,
    octs,
    fars,
    l7,
    l6,
    l5,
    l4,
    l3,
    c7f,
    c6f,
    c4f,
    own,
    halo,
    small,
    every,
    own_pick,
    hot_own,
    hot,
    hot_small,
    acc,
    d6,
    d7,
    load_sem,
    send_sem,
    recv_sem,
    all_send,
    all_recv,
):
    axes, counts, classes, nb4, nb3 = sizes
    n = counts[0] * counts[1]
    b7 = c7f.shape[1]
    b6 = b7 // 8
    b5 = b6 // 8
    per4 = 8 // b5
    block = b6 + 16
    me = lax.axis_index(axes[0]) * counts[1] + lax.axis_index(axes[1])

    def place(peer):
        return (peer // counts[1], peer % counts[1])

    loads = [
        pltpu.make_async_copy(src, dst, load_sem.at[k])
        for k, (src, dst) in enumerate(
            [
                (comp_h, comp),
                (mult_h, mult),
                (l7_h, l7),
                (l6_h, l6),
                (l5_h, l5),
                (l4_h, l4),
                (l3_h, l3),
                (octs_h, octs),
                (fars_h, fars),
            ]
        )
    ]
    for load in loads[:8]:
        load.start()

    barrier = pltpu.get_barrier_semaphore()

    def greet(k, carry):
        pl.semaphore_signal(
            barrier, inc=1, device_id=place(lax.rem(me + k, n)), device_id_type=MESH
        )
        return carry

    lax.fori_loop(1, n, greet, 0)
    c6f[...] = jnp.zeros_like(c6f)
    c4f[...] = jnp.zeros_like(c4f)
    rows3 = c4f.shape[1] // 8
    base4 = 3 * block
    base3 = base4 + nb4
    depth = small.shape[0]
    t4 = me // per4
    t3 = t4 // 8

    for k in range(2, 7):
        loads[k].wait()
    e7 = l7[...]
    p7 = jnp.where(e7 >= 0, e7 - (me * b7 - b7), -1).astype(F32).T.astype(jnp.int32)
    e6 = l6[...]
    p6 = e6 - (me * b6 - b6)
    p6 = p6 + jnp.where(p6 >= b6, block - b6, 0) + jnp.where(p6 >= 2 * b6, block - b6, 0)
    p6 = jnp.where(e6 >= 0, p6, -1).astype(F32)
    e5 = l5[...]
    p5 = e5 - (me * b5 - b5)
    p5 = p5 + b6 + jnp.where(p5 >= b5, block - b5, 0) + jnp.where(p5 >= 2 * b5, block - b5, 0)
    p5 = jnp.where(e5 >= 0, p5, -1)
    p5 = jnp.concatenate([p5, jnp.full((16 - b5, classes), -1, jnp.int32)], axis=0)

    e4 = l4[...]
    p4 = jnp.where(iota(e4.shape, 1) == t4, e4, -1).astype(F32)
    p4 = jnp.max(p4, axis=1, keepdims=True).astype(jnp.int32)
    p4 = jnp.where(p4 >= 0, p4 + base4, -1)
    e3 = l3[...]
    p3 = jnp.where(iota(e3.shape, 0) == t3, e3, -1).astype(F32)
    p3 = column(jnp.max(p3, axis=0, keepdims=True), classes).astype(jnp.int32)
    p3 = jnp.where(p3 >= 0, p3 + base3, -1)
    row = iota((16, 1), 0)

    group = 4
    lane7 = iota((b7, b7), 1).astype(jnp.int16)
    one, zero = jnp.ones((b7, b7), BF16), jnp.zeros((b7, b7), BF16)

    def build(c):
        col = jnp.broadcast_to(p7[:, c : c + 1], (b7, b7)).astype(jnp.int16)
        rows = pl.ds(c * b7, b7)
        hot_own[rows, :] = jnp.where(col == lane7 + b7, one, zero)
        hot[rows, 0:b7] = jnp.where(col == lane7, one, zero)
        hot[rows, b7 : 2 * b7] = jnp.where(col == lane7 + 2 * b7, one, zero)
        tail = jnp.where(row == b5, p4[c : c + 1, :], p5[:, c : c + 1])
        tail = jnp.where(row == b5 + 1, p3[c : c + 1, :], tail)
        cols = jnp.concatenate([column(p6[c : c + 1, :], b6).astype(jnp.int32), tail], axis=0)
        hot_small[c * block : (c + 1) * block, :] = onehot(cols, depth)

    for c in range(group):
        build(c)

    loads[0].wait()
    loads[1].wait()
    loads[8].start()
    seven = tn(mult[...], comp[...]).astype(BF16)
    own[...] = seven
    put_rows(c7f, 0, b7, seven.astype(F32))

    pl.semaphore_wait(barrier, n - 1)
    right = place(lax.rem(me + 1, n))
    left = place(lax.rem(me + n - 1, n))

    def halo_copy(src, ref, rows, slot, peer, index):
        return pltpu.make_async_remote_copy(
            src_ref=src,
            dst_ref=ref.at[pl.ds(slot * rows, rows), :],
            send_sem=send_sem.at[index],
            recv_sem=recv_sem.at[index],
            device_id=peer,
            device_id_type=MESH,
        )

    halo_sends = [
        halo_copy(own, halo, b7, 0, right, 0),
        halo_copy(own, halo, b7, 1, left, 1),
    ]
    for copy in halo_sends:
        copy.start()

    loads[7].wait()
    up = lanes_of(octs)
    six = nt(beside(take_rows(c7f, o, b6, 8).astype(BF16) for o in range(8)), up).astype(BF16)
    put_rows(c6f, 0, b6, six.astype(F32))
    five = nt(beside(take_rows(c6f, o, 16, 8).astype(BF16) for o in range(8)), up).astype(BF16)
    small[block : block + b6, :] = six
    small[block + b6 : 2 * block, :] = five
    fivef = five.astype(F32)
    half = octs.shape[1] // 2
    tile = jnp.concatenate([fivef[0:b5, :half], fivef[0:b5, half:]], axis=0)
    mine = pl.ds(pl.multiple_of(me * 8, 8), 8)
    every[mine, :] = tile

    small_sends = [
        halo_copy(small.at[pl.ds(block, block), :], small, block, 0, right, 2),
        halo_copy(small.at[pl.ds(block, block), :], small, block, 2, left, 3),
    ]

    def spread(k):
        pltpu.make_async_remote_copy(
            src_ref=every.at[mine, :],
            dst_ref=every.at[mine, :],
            send_sem=all_send,
            recv_sem=all_recv,
            device_id=place(lax.rem(me + k, n)),
            device_id_type=MESH,
        ).start()

    for copy in small_sends:
        copy.start()
    peers = iter(range(1, n))
    each = n - 1

    for c in range(classes):
        for k in itertools.islice(peers, each):
            spread(k)
        if c >= group:
            build(c)
        if c % group == group - 1:
            rows = pl.ds((c + 1 - group) * b7, group * b7)
            own_pick[rows, :] = nn(hot_own[rows, :], own[...]).astype(BF16)

    loads[8].wait()
    for copy in halo_sends:
        copy.wait_recv()

    def coarser():
        parts = []
        for o in range(8):
            at = (o // b5) * 8 + o % b5
            low = every[pl.ds(at, nb4, stride=8 * per4), :]
            high = every[pl.ds(at + b5, nb4, stride=8 * per4), :]
            parts += [low.astype(BF16), high.astype(BF16)]
        four = nt(beside(parts), up).astype(BF16)
        put_rows(c4f, 0, nb4, four.astype(F32))
        small[base4 : base4 + nb4, :] = four
        yield
        parts = [take_rows(c4f, o, rows3, 8).astype(BF16) for o in range(8)]
        small[base3 : base3 + rows3, :] = nt(beside(parts), up).astype(BF16)
        yield
        lesser = nn(hot_small[...], small[...]).astype(BF16)
        lesser = beside(lesser[c * block : (c + 1) * block, :] for c in range(classes))
        far = nt(lesser, lanes_of(fars))
        yield
        far6, far5 = 2.0 * far[0:b6, :], 4.0 * far[b6:block, :]
        far4 = 8.0 * far[b6 + b5 : b6 + b5 + 1, :]
        far3 = 16.0 * far[b6 + b5 + 1 : b6 + b5 + 2, :]
        wide = (16, octs.shape[1])
        down = nn(jnp.broadcast_to(far3, wide).astype(BF16), octs[t4 % 8])
        local4 = jnp.broadcast_to(far4 + down[0:1, :], wide)
        yield
        first = (me % per4) * b5
        parts = [jnp.where(iota(wide, 0) == k, local4, 0.0).astype(BF16) for k in range(b5)]
        ops = octs[pl.ds(first, b5)].reshape(b5 * wide[1], wide[1])
        local5 = far5 + nn(beside(parts), ops)
        local5 = local5.astype(BF16)
        yield
        for o in range(8):
            put_rows(d6, o, 8, nn(local5, octs[o])[0:8, :], 8)
        local6 = (far6 + take_rows(d6, 0, b6)).astype(BF16)
        yield
        for o in range(8):
            put_rows(d7, o, b6, nn(local6, octs[o]), 8)
            if o % 4 == 3:
                yield

    rest = every.at[pl.ds(0, (n - 1) * 8), :]
    chain = coarser()
    for start in range(0, classes, group):
        if start == group:
            pltpu.make_async_copy(rest, rest, all_recv).wait()
            for copy in small_sends:
                copy.wait_recv()
        if start >= group:
            next(chain, None)
        rows = pl.ds(start * b7, group * b7)
        picked = (nn(hot[rows, :], halo[...]) + own_pick[rows, :].astype(F32)).astype(BF16)
        if start >= group:
            next(chain, None)
        wide_picked = beside(picked[k * b7 : (k + 1) * b7, :] for k in range(group))
        far = nt(wide_picked, lanes_of(fars.at[pl.ds(start, group)]))
        acc[...] = far if start == 0 else acc[...] + far
    for _ in chain:
        pass
    local_ref[...] = (acc[...] + take_rows(d7, 0, b7)).astype(BF16)

    for copy in halo_sends + small_sends:
        copy.wait_send()
    pltpu.make_async_copy(rest, rest, all_send).wait()


def on_device(axes, counts, *args):
    mult, comp, expd, octs, fars, l7, l6, l5, l4, l3 = args
    args = (mult, comp.T, octs, fars, l7, l6, l5.T, l4, l3.T)
    n = counts[0] * counts[1]
    b7, b6, b5 = l7.shape[1], l6.shape[1], l5.shape[1]
    nb4, nb3 = l4.shape[1], l3.shape[1]
    classes, r = fars.shape[0], fars.shape[1]
    if b6 * 8 != b7 or b5 * 8 != b6 or b5 != 4 or nb4 % 16:
        raise ValueError("unsupported sizes")
    block = b6 + 16
    rows3 = max(16, nb3)
    depth = 3 * block + nb4 + rows3
    scratch = [pltpu.VMEM(a.shape, a.dtype) for a in args]
    scratch += [
        pltpu.VMEM((r // 128, b7, 128), F32),
        pltpu.VMEM((r // 128, 128, 128), F32),
        pltpu.VMEM((r // 128, rows3 * 8, 128), F32),
        pltpu.VMEM((b7, r), BF16),
        pltpu.VMEM((2 * b7, r), BF16),
        pltpu.VMEM((depth, r), BF16),
        pltpu.VMEM((n * 8, r // 2), F32),
        pltpu.VMEM((classes * b7, r), BF16),
        pltpu.VMEM((classes * b7, b7), BF16),
        pltpu.VMEM((classes * b7, 2 * b7), BF16),
        pltpu.VMEM((classes * block, depth), BF16),
        pltpu.VMEM((b7, r), F32),
        pltpu.VMEM((r // 128, 64, 128), F32),
        pltpu.VMEM((r // 128, b7, 128), F32),
        pltpu.SemaphoreType.DMA((9,)),
        pltpu.SemaphoreType.DMA((4,)),
        pltpu.SemaphoreType.DMA((4,)),
        pltpu.SemaphoreType.DMA,
        pltpu.SemaphoreType.DMA,
    ]
    local = pl.pallas_call(
        functools.partial(kernel, (axes, counts, classes, nb4, nb3)),
        out_shape=pltpu.VMEM((b7, r), BF16),
        in_specs=[pl.BlockSpec(memory_space=pltpu.HBM)] * len(args),
        out_specs=pl.BlockSpec(memory_space=pltpu.VMEM),
        scratch_shapes=scratch,
        compiler_params=pltpu.CompilerParams(
            collective_id=0, has_side_effects=True, vmem_limit_bytes=50 * 1024 * 1024
        ),
    )(*[pltpu.with_memory_space_constraint(a, pltpu.HBM) for a in args])
    return nt(expd, local)


def solution(mesh):
    axes = tuple(mesh.axis_names)
    counts = tuple(mesh.shape[a] for a in axes)
    cut = P(None, axes)
    return jax.shard_map(
        functools.partial(on_device, axes, counts),
        mesh=mesh,
        in_specs=(cut, P(), P(), P(), P(), cut, cut, cut, P(), P()),
        out_specs=cut,
        check_vma=False,
    )
```
